256 devices in a mesh: strip: 32 (over x, z), band: 8 (over y, core).
Axes of the slice: x: 4, y: 4, z: 8, core: 2. Of those that a mesh axis runs over, the one named last changes fastest.
Arguments:
- state: float32 [128, 4, 4, 128, 1024], P(None, None, None, 'strip', 'band'), may hold values from -8 to 8
- wind_x: float32 [4, 4, 128, 1024], P(None, None, 'strip', 'band'), may hold values from -6 to 6
- wind_y: float32 [4, 4, 128, 1024], P(None, None, 'strip', 'band'), may hold values from -6 to 6
- jacobian: float32 [4, 4, 128, 1024], P(None, None, 'strip', 'band'), may hold values from 0.5 to 2
- to_physics: float32 [4, 16], replicated, may hold values from 0 to 0.125
- to_dynamics: float32 [16, 4], replicated, may hold values from 0 to 0.5
- feature_mean: float32 [128], replicated, may hold values from -1.5 to 1.5
- feature_scale: float32 [128], replicated, may hold values from 0.5 to 2
- w_in: bfloat16 [128, 512], replicated, may hold values from -0.5 to 0.5
- w_hidden: bfloat16 [4, 512, 512], replicated, may hold values from -0.25 to 0.25
- w_out: bfloat16 [512, 128], replicated, may hold values from -0.25 to 0.25
- bias_hidden: float32 [5, 512], replicated, may hold values from -1.5 to 1.5
- bias_out: float32 [128], replicated, may hold values from -1.5 to 1.5
- live_counts: int32 [32, 8], replicated, may hold values from 256 to 2048, as said below
Outputs:
- new_state: float32 [128, 4, 4, 128, 1024], P(None, None, None, 'strip', 'band')
The draws below stay inside these ranges and needn't reach their ends.
Inputs may be any that keep to these rules, and one draw needn't show every extreme that they name: `live_counts`: for every band index some strip index has all 2048 columns live.
All inputs are finite; a program needn't handle non-finite values.
Results may differ from the reference program's by a relative error of at most 0.0009.
Values may be sent and summed in bfloat16 or wider, within the bound.
A program may use at most 128 MiB of HBM per device.

```python
import math
import jax
import jax.numpy as jnp
import numpy as np
from jax import lax

F = 128
HID = 512
DEPTH = 4
EX = 4
EY = 128
COLS = 2048
NEX = 128
NEY = 1024
STRIPS = 32
BANDS = 8


def draw_live_counts(key, part):
    key = jax.random.fold_in(key, 11)
    first_key, second_key = jax.random.split(key)
    base = jax.random.randint(first_key, (STRIPS, BANDS), COLS // 8, COLS // 2 + 1)
    full = jax.random.randint(second_key, (BANDS,), 0, STRIPS)
    chosen = jnp.arange(STRIPS)[:, None] == full[None, :]
    return jnp.where(chosen, COLS, base).astype(jnp.int32)


def shard_levels(stream_key, shape, pieces, least, top_value):
    level = 1.0
    for position, parts in pieces:
        heights = jax.random.uniform(jax.random.fold_in(jax.random.fold_in(stream_key, 6), position), (parts,), jnp.float32, least / len(pieces), top_value / len(pieces))
        level = level * jnp.repeat(jnp.exp(heights), shape[position] // parts).reshape((-1,) + (1,) * (len(shape) - 1 - position))
    return level


def scatter_about(stream_key, shape, spread, bound, pieces=(), kind=jnp.bfloat16):
    gain = shard_levels(stream_key, shape, pieces, -0.22, 0.18) if pieces else 1.0
    values = jax.random.normal(stream_key, shape, jnp.float32) * spread * gain
    return jnp.minimum(jnp.maximum(values, -bound), bound).astype(kind)


def setup_inputs(seed: int = 0) -> dict:
    streams_of = jax.random.split(jax.random.key(seed), 15)
    state = scatter_about(streams_of[0], (F, 4, 4, NEX, NEY), 1.0, 8.0, ((3, 32), (4, 8)), jnp.float32)
    wind_x = scatter_about(streams_of[1], (4, 4, NEX, NEY), 1.0, 6.0, ((2, 32), (3, 8)), jnp.float32)
    wind_y = scatter_about(streams_of[2], (4, 4, NEX, NEY), 1.0, 6.0, ((2, 32), (3, 8)), jnp.float32)
    jacobian = jnp.clip(jnp.exp(math.log(2.0) - 1.3862944 * jax.random.uniform(streams_of[3], (4, 4, NEX, NEY), jnp.float32) ** shard_levels(streams_of[3], (4, 4, NEX, NEY), ((2, 32), (3, 8)), -0.2, 0.2)), 0.5, 2.0)
    to_physics = jnp.clip(jax.random.uniform(streams_of[4], (4, 16), jnp.float32, 0.0, 0.125), 0.0, 0.125)
    to_dynamics = jnp.clip(jax.random.uniform(streams_of[5], (16, 4), jnp.float32, 0.0, 0.5), 0.0, 0.5)
    feature_mean = scatter_about(streams_of[6], (F,), 0.3, 1.5, (), jnp.float32)
    feature_scale = jnp.clip(jnp.exp(jax.random.uniform(streams_of[7], (F,), jnp.float32, math.log(0.5), math.log(2.0))), 0.5, 2.0)
    w_in = scatter_about(streams_of[8], (F, HID), F ** -0.5, 0.5)
    w_hidden = scatter_about(streams_of[9], (DEPTH, HID, HID), HID ** -0.5, 0.25)
    w_out = scatter_about(streams_of[10], (HID, F), HID ** -0.5, 0.25)
    bias_hidden = scatter_about(streams_of[11], (DEPTH + 1, HID), 0.3, 1.5, (), jnp.float32)
    bias_out = scatter_about(streams_of[12], (F,), 0.3, 1.5, (), jnp.float32)
    live_counts = draw_live_counts(jax.random.fold_in(streams_of[14], 71), 0)
    return dict(state=state, wind_x=wind_x, wind_y=wind_y, jacobian=jacobian, to_physics=to_physics, to_dynamics=to_dynamics, feature_mean=feature_mean, feature_scale=feature_scale, w_in=w_in, w_hidden=w_hidden, w_out=w_out, bias_hidden=bias_hidden, bias_out=bias_out, live_counts=live_counts)


step_size = 0.1
slope = 0.15

def gll_tables():
    nodes = np.array([-1.0, -1.0 / np.sqrt(5.0), 1.0 / np.sqrt(5.0), 1.0])
    weights = np.array([1.0 / 6.0, 5.0 / 6.0, 5.0 / 6.0, 1.0 / 6.0])
    derivative = np.zeros((4, 4))
    for first in range(4):
        for second in range(4):
            if first != second:
                top = np.prod([nodes[first] - nodes[other] for other in range(4) if other != first])
                bottom = np.prod([nodes[second] - nodes[other] for other in range(4) if other != second])
                derivative[first, second] = top / (bottom * (nodes[first] - nodes[second]))
            else:
                derivative[first, first] = np.sum([1.0 / (nodes[first] - nodes[other]) for other in range(4) if other != first])
    return (weights, derivative)

def column_network(rows, w_in, w_hidden, w_out, bias_hidden, bias_out):
    hidden = jax.nn.leaky_relu(jnp.dot(rows, w_in, preferred_element_type=jnp.float32) + bias_hidden[0], slope).astype(jnp.bfloat16)
    for layer in range(w_hidden.shape[0]):
        hidden = jax.nn.leaky_relu(jnp.dot(hidden, w_hidden[layer], preferred_element_type=jnp.float32) + bias_hidden[layer + 1], slope).astype(jnp.bfloat16)
    return (jnp.dot(hidden, w_out, preferred_element_type=jnp.float32) + bias_out).astype(jnp.bfloat16)

def reference(state, wind_x, wind_y, jacobian, to_physics, to_dynamics, feature_mean, feature_scale, w_in, w_hidden, w_out, bias_hidden, bias_out, live_counts):
    highest = lax.Precision.HIGHEST
    feats = state.shape[0]
    weights, derivative = gll_tables()
    table = jnp.asarray(derivative, jnp.float32)
    along_i = jnp.einsum('ab,fbjxy->fajxy', table, state, precision=highest)
    along_j = jnp.einsum('ab,fibxy->fiaxy', table, state, precision=highest)
    advected = state - step_size * (wind_x * along_i + wind_y * along_j)
    quad = jnp.asarray(np.outer(weights, weights), jnp.float32)
    mass = quad[:, :, None, None] * jacobian
    packed_q = jnp.concatenate([mass * advected, mass[None]], 0)
    along_x = packed_q.at[:, 0].add(jnp.roll(packed_q[:, 3], 1, axis=2)).at[:, 3].add(jnp.roll(packed_q[:, 0], -1, axis=2))
    along_y = along_x.at[:, :, 0].add(jnp.roll(along_x[:, :, 3], 1, axis=3)).at[:, :, 3].add(jnp.roll(along_x[:, :, 0], -1, axis=3))
    assembled = along_y[:feats] / along_y[feats][None]
    columns = jnp.einsum('cn,fnxy->cxyf', to_physics, assembled.reshape(feats, 16, NEX, NEY), precision=highest)
    physics_in = ((columns - feature_mean) * feature_scale).astype(jnp.bfloat16)
    rows = physics_in.reshape(-1, feats)
    total = rows.shape[0]
    block = math.gcd(total, 4096)
    raw = lax.map(lambda part_rows: column_network(part_rows, w_in, w_hidden, w_out, bias_hidden, bias_out), rows.reshape(total // block, block, feats))
    raw = raw.reshape(4, NEX, NEY, feats)
    cell = lax.broadcasted_iota(jnp.int32, (4, NEX, NEY), 0)
    xpos = lax.broadcasted_iota(jnp.int32, (4, NEX, NEY), 1)
    ypos = lax.broadcasted_iota(jnp.int32, (4, NEX, NEY), 2)
    local_number = cell * (EX * EY) + xpos % EX * EY + ypos % EY
    limits = live_counts[xpos // EX, ypos // EY]
    tendency = jnp.where((local_number < limits)[..., None], raw, jnp.zeros_like(raw))
    back = jnp.einsum('nc,cxyf->fnxy', to_dynamics, tendency.astype(jnp.float32), precision=highest)
    return assembled + back.reshape(feats, 4, 4, NEX, NEY)
```

```python
import jax
import jax.numpy as jnp
import numpy as np
from jax import lax
from jax.experimental import pallas as pl
from jax.experimental.pallas import tpu as pltpu
from jax.sharding import PartitionSpec as P

MESH = pl.DeviceIdType.MESH
step_size = 0.1
slope = 0.15
F32 = jnp.float32
BF16 = jnp.bfloat16


def gll_tables():
    nodes = np.array([-1.0, -1.0 / np.sqrt(5.0), 1.0 / np.sqrt(5.0), 1.0])
    weights = np.array([1.0 / 6.0, 5.0 / 6.0, 5.0 / 6.0, 1.0 / 6.0])
    derivative = np.zeros((4, 4))
    for first in range(4):
        for second in range(4):
            if first != second:
                top = np.prod([nodes[first] - nodes[other] for other in range(4) if other != first])
                bottom = np.prod(
                    [nodes[second] - nodes[other] for other in range(4) if other != second]
                )
                derivative[first, second] = top / (bottom * (nodes[first] - nodes[second]))
            else:
                derivative[first, first] = np.sum(
                    [1.0 / (nodes[first] - nodes[other]) for other in range(4) if other != first]
                )
    return (weights, derivative)


WEIGHTS, DERIV = gll_tables()
QUAD = np.outer(WEIGHTS, WEIGHTS)
EVEN = [(DERIV[r, 0] + DERIV[r, 3]) / 2 for r in (0, 1)]
ODD0 = [(DERIV[r, 0] - DERIV[r, 3]) / 2 for r in (0, 1)]
ODD1 = [(DERIV[r, 1] - DERIV[r, 2]) / 2 for r in (0, 1)]
LEAD = [ODD0[0], ODD1[1], ODD1[1], ODD0[0]]


def mirrored(s0, s1, s2, s3):
    even = (s0 + s3) - (s1 + s2)
    far, near = s0 - s3, s1 - s2
    outer = far + F32(ODD1[0] / ODD0[0]) * near
    inner = near + F32(ODD0[1] / ODD1[1]) * far
    outer_e = F32(EVEN[0] / ODD0[0]) * even
    inner_e = F32(EVEN[1] / ODD1[1]) * even
    return outer + outer_e, inner + inner_e, inner - inner_e, outer - outer_e


def lanes(rows):
    return lax.broadcasted_iota(jnp.int32, (rows, 128), 1)


def exchange_kernel(
    n_strip, n_band,
    state, wind_x, wind_y, jac, to_phys, to_dyn, mean, scale, w_in, w_hidden, w_out, bias_h, bias_o, counts,
    a_out, wi_out, wh_out, wo_out, bh_out, bo_out, tab_out, norm_out, cnt_out,
    sbuf, wxv, wyv, jacv, coef, qbuf, edge_send, edge_recv, pack, pick, ysend, yrecv,
    jstrip, jband, jdiag, gather, halo, rmass, tp_s, td_s, cnt_s, rowv,
    in_sem, small_sem, w_sem, send_sem, recv_sem,
):
    s = lax.axis_index("strip")
    b = lax.axis_index("band")
    sp, sm = lax.rem(s + 1, n_strip), lax.rem(s + n_strip - 1, n_strip)
    bp, bm = lax.rem(b + 1, n_band), lax.rem(b + n_band - 1, n_band)

    barrier = pltpu.get_barrier_semaphore()
    for dev in ((sp, b), (sm, b), (s, bp), (s, bm), (sp, bp), (sp, bm), (sm, bp), (sm, bm)):
        pl.semaphore_signal(barrier, inc=1, device_id=dev, device_id_type=MESH)

    def local(src, dst, sem):
        c = pltpu.make_async_copy(src, dst, sem)
        c.start()
        return c

    jac_in = local(jac, jacv, small_sem.at[0])
    wx_in = local(wind_x, wxv, small_sem.at[1])
    wy_in = local(wind_y, wyv, small_sem.at[2])

    def state_copy(k):
        at = pl.ds(k * 1024 if isinstance(k, int) else pl.multiple_of(k * 1024, 1024), 1024)
        return pltpu.make_async_copy(state.at[at], sbuf.at[at], in_sem.at[k])

    for k in range(8):
        state_copy(k).start()
    later = [
        local(to_phys, tp_s, small_sem.at[3]),
        local(to_dyn, td_s, small_sem.at[4]),
        local(counts, cnt_s, small_sem.at[5]),
        local(mean, rowv.at[0], small_sem.at[6]),
        local(scale, rowv.at[1], small_sem.at[7]),
        local(bias_h, bh_out, small_sem.at[8]),
        local(bias_o, bo_out, small_sem.at[9]),
    ]
    w_in_copies = [
        local(w_in, wi_out, w_sem.at[0]),
        local(w_hidden, wh_out, w_sem.at[1]),
        local(w_out, wo_out, w_sem.at[2]),
    ]

    jac_in.wait()
    pl.semaphore_wait(barrier, 8)

    copies = []

    def remote(src, dst, dev):
        n = len(copies)
        c = pltpu.make_async_remote_copy(
            src_ref=src, dst_ref=dst, send_sem=send_sem.at[n], recv_sem=recv_sem.at[n],
            device_id=dev, device_id_type=MESH,
        )
        copies.append(c)
        return c

    top, low = pl.ds(8, 8), pl.ds(0, 8)
    jac_copies = [
        remote(jacv.at[3], jstrip.at[0], (sp, b)),
        remote(jacv.at[0], jstrip.at[1], (sm, b)),
        remote(jacv.at[:, top], jband.at[0], (s, bp)),
        remote(jacv.at[:, low], jband.at[1], (s, bm)),
        remote(jacv.at[3, top], jdiag.at[0], (sp, bp)),
        remote(jacv.at[3, low], jdiag.at[1], (sp, bm)),
        remote(jacv.at[0, top], jdiag.at[2], (sm, bp)),
        remote(jacv.at[0, low], jdiag.at[3], (sm, bm)),
    ]
    for c in jac_copies:
        c.start()
    halves = [pl.ds(0, 64), pl.ds(64, 64)]
    edge_copies = [
        [
            remote(edge_send.at[0, :, h], edge_recv.at[0, :, h], (sp, b)),
            remote(edge_send.at[1, :, h], edge_recv.at[1, :, h], (sm, b)),
        ]
        for h in halves
    ]
    y_copies = [
        remote(ysend, yrecv.at[0], (s, bp)),
        remote(ysend, yrecv.at[1], (s, bm)),
        remote(ysend, yrecv.at[2], (sp, bp)),
        remote(ysend, yrecv.at[3], (sp, bm)),
        remote(ysend, yrecv.at[4], (sm, bp)),
        remote(ysend, yrecv.at[5], (sm, bm)),
    ]

    wide = (32, 2048)
    row, col = (lax.broadcasted_iota(jnp.int32, wide, d) for d in (0, 1))
    at = (row // 2) * 128 + jnp.where(lax.rem(row, 2) == 0, 127, 0)
    pick[...] = jnp.where(col == at, F32(1.0), F32(0.0)).astype(BF16)

    wx_in.wait()
    wy_in.wait()
    for i in range(4):
        for jp in range(2):
            at = slice(i * 16 + jp * 8, i * 16 + jp * 8 + 8)
            first = lax.broadcasted_iota(jnp.int32, (8, 128), 0) < 4
            j0, j1 = 2 * jp, 2 * jp + 1
            m = jacv[i, jp * 8:jp * 8 + 8] * jnp.where(first, F32(QUAD[i, j0]), F32(QUAD[i, j1]))
            coef[0, at] = m
            coef[1, at] = m * wxv[at] * F32(-step_size * LEAD[i])
            lead = jnp.where(first, F32(-step_size * LEAD[j0]), F32(-step_size * LEAD[j1]))
            coef[2, at] = m * wyv[at] * lead

    lane8 = lanes(8)

    def advect(k, carry):
        state_copy(k).wait()
        for g in range(2):
            f0 = pl.multiple_of(k * 16 + g * 8, 8)
            fs = pl.ds(f0, 8)
            for x in range(4):
                v = [[sbuf[pl.ds(f0 * 64 + (i * 16 + j * 4 + x), 8, stride=64), :] for j in range(4)] for i in range(4)]
                q = [[None] * 4 for _ in range(4)]
                for j in range(4):
                    d = mirrored(*[v[i][j] for i in range(4)])
                    for i in range(4):
                        r = i * 16 + j * 4 + x
                        q[i][j] = coef[0, r:r + 1] * v[i][j] + coef[1, r:r + 1] * d[i]
                for i in range(4):
                    d = mirrored(*v[i])
                    for j in range(4):
                        r = i * 16 + j * 4 + x
                        q[i][j] = q[i][j] + coef[2, r:r + 1] * d[j]
                        qbuf[r, fs, :] = q[i][j]
                    n = i * 4 + x
                    pack[fs, n * 128:n * 128 + 128] = jnp.where(lane8 == 127, q[i][3], q[i][0])
        return carry

    for half in range(2):
        lax.fori_loop(half * 4, half * 4 + 4, advect, 0)
        fs = halves[half]
        for j in range(4):
            edge_send[0, j, fs, :] = qbuf[48 + j * 4 + 3, fs, :].astype(BF16)
            edge_send[1, j, fs, :] = qbuf[j * 4, fs, :].astype(BF16)
        for c in edge_copies[half]:
            c.start()
    ysend[...] = lax.dot_general(
        pick[...], pack[...].astype(BF16), (((1,), (1,)), ((), ())), preferred_element_type=F32
    ).astype(BF16)
    for c in y_copies:
        c.start()

    for c in later:
        c.wait()
    for c in range(4):
        for n in range(16):
            tab_out[0, pl.ds(c * 16 + n, 1)] = jnp.full((1, 128), tp_s[c, n], F32)
            tab_out[1, pl.ds(c * 16 + n, 1)] = jnp.full((1, 128), td_s[c, n], F32)
    norm_out[0] = jnp.broadcast_to(rowv[0:1], (128, 128)).T
    norm_out[1] = jnp.broadcast_to(rowv[1:2], (128, 128)).T
    cnt_out[...] = jnp.full((8, 128), cnt_s[b, s], jnp.int32)

    for c in jac_copies:
        c.wait()
    lane1 = lanes(1)

    def element(side, i, j, x):
        w = F32(QUAD[i, j])
        r = j * 4 + x
        if side is None:
            return coef[0, i * 16 + r:i * 16 + r + 1]
        return w * jband[side, i, (r - 8 if side == 0 else r):(r - 8 if side == 0 else r) + 1]

    def outer(strip_side, band_side, j):
        i, x = (3, 3) if strip_side == 0 else (0, 0)
        w = F32(QUAD[i, j])
        r = j * 4 + x
        if band_side is None:
            return w * jstrip[strip_side, r:r + 1]
        r = r - 8 if band_side == 0 else r
        return w * jdiag[strip_side * 2 + band_side, r:r + 1]

    def level_mass(level, side, j):
        if level == 0:
            return element(side, 0, j, 0) + outer(0, side, j)
        if level == 12:
            return element(side, 3, j, 3) + outer(1, side, j)
        x, i = divmod(level, 3)
        if i == 0:
            return element(side, 0, j, x) + element(side, 3, j, x - 1)
        return element(side, i, j, x)

    for level in range(13):
        m = [level_mass(level, None, j) for j in range(4)]
        before = jnp.where(lane1 == 127, level_mass(level, 0, 3), m[3])
        after = jnp.where(lane1 == 0, level_mass(level, 1, 0), m[0])
        totals = [m[0] + pltpu.roll(before, 1, 1), m[1], m[2], m[3] + pltpu.roll(after, 127, 1)]
        for j in range(4):
            rmass[pl.ds(level * 4 + j, 1)] = 1.0 / totals[j]

    for c in y_copies:
        c.wait()
    odd = lax.rem(lax.broadcasted_iota(jnp.int32, (32, 128), 0), 2) == 1
    for t in range(3):
        from_left = pltpu.roll(yrecv[2 * t].astype(F32), 1, 0)
        from_right = pltpu.roll(yrecv[2 * t + 1].astype(F32), 31, 0)
        gather[t * 32:(t + 1) * 32] = jnp.where(odd, from_left, from_right)

    def pair(t, i, x):
        r = t * 32 + 2 * (i * 4 + x)
        return gather[r:r + 2]

    rows = []
    for level in range(13):
        x, i = divmod(level, 3)
        if level == 0:
            rows.append(pair(0, 0, 0) + pair(1, 3, 3))
        elif level == 12:
            rows.append(pair(0, 3, 3) + pair(2, 0, 0))
        elif i == 0:
            rows.append(pair(0, 0, x) + pair(0, 3, x - 1))
        else:
            rows.append(pair(0, i, x))
    halo[...] = jnp.zeros((128, 128), F32)
    for level in range(13):
        halo[2 * level:2 * level + 2] = rows[level]
    halo[...] = halo[...].T

    for group in edge_copies:
        for c in group:
            c.wait()

    lane16 = lanes(16)

    def assemble(k, carry):
        fs = pl.ds(pl.multiple_of(k * 16, 16), 16)
        h = halo[fs, :]
        for level in range(13):
            x, i = divmod(level, 3)
            v = []
            for j in range(4):
                if level == 12:
                    u = qbuf[48 + j * 4 + 3, fs, :] + edge_recv[1, j, fs, :].astype(F32)
                else:
                    u = qbuf[i * 16 + j * 4 + x, fs, :]
                    if level == 0:
                        u = u + edge_recv[0, j, fs, :].astype(F32)
                    elif i == 0:
                        u = u + qbuf[48 + j * 4 + x - 1, fs, :]
                v.append(u)
            hr = pltpu.roll(h, 128 - (2 * level + 1), 1)
            first = v[0] + jnp.where(lane16 == 0, hr, pltpu.roll(v[3], 1, 1))
            last = v[3] + jnp.where(lane16 == 127, hr, pltpu.roll(v[0], 127, 1))
            for j, u in enumerate((first, v[1], v[2], last)):
                p = level * 4 + j
                a_out[p, fs, :] = u * rmass[p:p + 1]
        return carry

    lax.fori_loop(0, 8, assemble, 0)
    for c in w_in_copies:
        c.wait()


def physics_kernel(a, wi, wh, wo, bh, bo, tab, norm, cnt, out, xt, tend, obuf, out_sem):
    def act(acc, bias):
        v = acc + bias
        return jnp.maximum(v, F32(slope) * v).astype(BF16)

    lane = lanes(1)
    copies = []
    for x in range(4):
        def columns(k, carry):
            fs = pl.ds(pl.multiple_of(k * 16, 16), 16)
            acc = [None] * 4
            for n in range(16):
                v = a[(3 * x + n // 4) * 4 + n % 4, fs, :]
                for c in range(4):
                    t = tab[0, c * 16 + n:c * 16 + n + 1] * v
                    acc[c] = t if acc[c] is None else acc[c] + t
            for c in range(4):
                v = (acc[c] - norm[0, fs, :]) * norm[1, fs, :]
                xt[fs, c * 128:(c + 1) * 128] = v.astype(BF16)
            return carry

        lax.fori_loop(0, 8, columns, 0)
        h = act(jnp.dot(xt[...].T, wi[...], preferred_element_type=F32), bh[0:1])
        for layer in range(4):
            h = act(jnp.dot(h, wh[layer], preferred_element_type=F32), bh[layer + 1:layer + 2])
        raw = (jnp.dot(h, wo[...], preferred_element_type=F32) + bo[...]).astype(BF16)
        raw = raw.T
        for c in range(4):
            live = lane + (c * 512 + x * 128) < cnt[0:1]
            part = raw[:, c * 128:(c + 1) * 128].astype(F32)
            tend[c] = jnp.where(live, part, F32(0.0))

        def back(k, carry):
            fs = pl.ds(pl.multiple_of(k * 16, 16), 16)
            t = [tend[c, fs, :] for c in range(4)]
            for n in range(16):
                v = a[(3 * x + n // 4) * 4 + n % 4, fs, :]
                for c in range(4):
                    v = v + tab[1, c * 16 + n:c * 16 + n + 1] * t[c]
                obuf[x, n, fs, :] = v
            return carry

        lax.fori_loop(0, 8, back, 0)
        for n in range(16):
            c = pltpu.make_async_copy(obuf.at[x, n], out.at[:, n * 4 + x, :], out_sem.at[x * 16 + n])
            c.start()
            copies.append(c)
    for c in copies:
        c.wait()


def body(
    state, wind_x, wind_y, jacobian, to_physics, to_dynamics, feature_mean, feature_scale,
    w_in, w_hidden, w_out, bias_hidden, bias_out, live_counts,
):
    n_strip, n_band = lax.axis_size("strip"), lax.axis_size("band")
    hbm = pl.BlockSpec(memory_space=pltpu.HBM)
    vmem = pl.BlockSpec(memory_space=pltpu.VMEM)
    args = (
        state.reshape(8192, 128), wind_x.reshape(64, 128), wind_y.reshape(64, 128),
        jacobian.reshape(4, 16, 128), to_physics, to_dynamics.T, feature_mean, feature_scale,
        w_in, w_hidden, w_out, bias_hidden, bias_out.reshape(1, 128), live_counts.T,
    )
    args = [pltpu.with_memory_space_constraint(v, pltpu.HBM) for v in args]
    dma = pltpu.SemaphoreType.DMA
    made = pl.pallas_call(
        lambda *refs: exchange_kernel(n_strip, n_band, *refs),
        out_shape=[
            pltpu.VMEM((52, 128, 128), F32),
            pltpu.VMEM((128, 512), BF16),
            pltpu.VMEM((4, 512, 512), BF16),
            pltpu.VMEM((512, 128), BF16),
            pltpu.VMEM((5, 512), F32),
            pltpu.VMEM((1, 128), F32),
            pltpu.VMEM((2, 64, 128), F32),
            pltpu.VMEM((2, 128, 128), F32),
            pltpu.VMEM((8, 128), jnp.int32),
        ],
        in_specs=[hbm] * len(args),
        out_specs=[vmem] * 9,
        scratch_shapes=[
            pltpu.VMEM((8192, 128), F32),
            pltpu.VMEM((64, 128), F32),
            pltpu.VMEM((64, 128), F32),
            pltpu.VMEM((4, 16, 128), F32),
            pltpu.VMEM((3, 64, 128), F32),
            pltpu.VMEM((64, 128, 128), F32),
            pltpu.VMEM((2, 4, 128, 128), BF16),
            pltpu.VMEM((2, 4, 128, 128), BF16),
            pltpu.VMEM((128, 2048), F32),
            pltpu.VMEM((32, 2048), BF16),
            pltpu.VMEM((32, 128), BF16),
            pltpu.VMEM((6, 32, 128), BF16),
            pltpu.VMEM((2, 16, 128), F32),
            pltpu.VMEM((2, 4, 8, 128), F32),
            pltpu.VMEM((4, 8, 128), F32),
            pltpu.VMEM((96, 128), F32),
            pltpu.VMEM((128, 128), F32),
            pltpu.VMEM((52, 128), F32),
            pltpu.SMEM((4, 16), F32),
            pltpu.SMEM((4, 16), F32),
            pltpu.SMEM((n_band, n_strip), jnp.int32),
            pltpu.VMEM((2, 128), F32),
            dma((8,)),
            dma((10,)),
            dma((3,)),
            dma((18,)),
            dma((18,)),
        ],
        name="exchange",
        compiler_params=pltpu.CompilerParams(
            collective_id=0, has_side_effects=True, vmem_limit_bytes=28 << 20
        ),
    )(*args)
    out = pl.pallas_call(
        physics_kernel,
        out_shape=jax.ShapeDtypeStruct((128, 64, 128), F32),
        in_specs=[vmem] * 9,
        out_specs=hbm,
        scratch_shapes=[
            pltpu.VMEM((128, 512), BF16),
            pltpu.VMEM((4, 128, 128), F32),
            pltpu.VMEM((4, 16, 128, 128), F32),
            dma((64,)),
        ],
        name="physics",
        compiler_params=pltpu.CompilerParams(vmem_limit_bytes=28 << 20),
    )(*made)
    return out.reshape(state.shape)


def solution(mesh):
    placed = (
        P(None, None, None, "strip", "band"),
        P(None, None, "strip", "band"),
        P(None, None, "strip", "band"),
        P(None, None, "strip", "band"),
        P(), P(), P(), P(), P(), P(), P(), P(), P(), P(),
    )
    return jax.shard_map(
        body,
        mesh=mesh,
        in_specs=placed,
        out_specs=P(None, None, None, "strip", "band"),
        check_vma=False,
    )
```

```python
import jax
import jax.numpy as jnp
import numpy as np
from jax import lax
from jax.experimental import pallas as pl
from jax.experimental.pallas import tpu as pltpu
from jax.sharding import PartitionSpec as P

MESH = pl.DeviceIdType.MESH
step_size = 0.1
slope = 0.15
F32 = jnp.float32
BF16 = jnp.bfloat16


def gll_tables():
    nodes = np.array([-1.0, -1.0 / np.sqrt(5.0), 1.0 / np.sqrt(5.0), 1.0])
    weights = np.array([1.0 / 6.0, 5.0 / 6.0, 5.0 / 6.0, 1.0 / 6.0])
    derivative = np.zeros((4, 4))
    for first in range(4):
        for second in range(4):
            if first != second:
                top = np.prod([nodes[first] - nodes[other] for other in range(4) if other != first])
                bottom = np.prod(
                    [nodes[second] - nodes[other] for other in range(4) if other != second]
                )
                derivative[first, second] = top / (bottom * (nodes[first] - nodes[second]))
            else:
                derivative[first, first] = np.sum(
                    [1.0 / (nodes[first] - nodes[other]) for other in range(4) if other != first]
                )
    return (weights, derivative)


WEIGHTS, DERIV = gll_tables()
QUAD = np.outer(WEIGHTS, WEIGHTS)
EVEN = [(DERIV[r, 0] + DERIV[r, 3]) / 2 for r in (0, 1)]
ODD0 = [(DERIV[r, 0] - DERIV[r, 3]) / 2 for r in (0, 1)]
ODD1 = [(DERIV[r, 1] - DERIV[r, 2]) / 2 for r in (0, 1)]
LEAD = [ODD0[0], ODD1[1], ODD1[1], ODD0[0]]


def mirrored(s0, s1, s2, s3):
    even = (s0 + s3) - (s1 + s2)
    far, near = s0 - s3, s1 - s2
    outer = far + F32(ODD1[0] / ODD0[0]) * near
    inner = near + F32(ODD0[1] / ODD1[1]) * far
    outer_e = F32(EVEN[0] / ODD0[0]) * even
    inner_e = F32(EVEN[1] / ODD1[1]) * even
    return outer + outer_e, inner + inner_e, inner - inner_e, outer - outer_e


def lanes(rows):
    return lax.broadcasted_iota(jnp.int32, (rows, 128), 1)


def columns_part(a_of, tab, levels, nodes, fs, acc):
    for i, level in levels:
        for j in nodes:
            v = a_of(level * 4 + j, fs)
            for c in range(4):
                r = c * 16 + i * 4 + j
                term = tab[0, r:r + 1] * v
                acc[c] = term if acc[c] is None else acc[c] + term
    return acc


def network(xt, wi, wh, wo, bh, bo, cnt, tend, xs, parts):
    lane = lanes(1).astype(F32)

    def act(acc, bias):
        v = acc + bias
        return jnp.maximum(v, F32(slope) * v).astype(BF16)

    def dot(p, q):
        return jnp.dot(p, q, preferred_element_type=F32)

    hs = [act(dot(xt[:, p * 512:(p + 1) * 512].T, wi[...]), bh[0:1]) for p in parts]
    for layer in range(4):
        hs = [act(dot(h, wh[layer]), bh[layer + 1:layer + 2]) for h in hs]
    for p, h in zip(parts, hs):
        raw = (dot(h, wo[...]) + bo[...]).astype(BF16).T
        for cell in range(2):
            for g in range(2):
                c = 2 * p + cell
                live = lane + F32(c * 512 + xs[g] * 128) < cnt[0:1]
                at = (cell * 2 + g) * 128
                tend[g, c] = jnp.where(live, raw[:, at:at + 128].astype(F32), F32(0.0))


def back_loop(a, tab, tend, g, x, cells, store):
    def back(k, carry):
        fs = pl.ds(pl.multiple_of(k * 16, 16), 16)
        t = [tend[g, c, fs, :] for c in range(cells)]
        for n in range(16):
            v = a[(3 * x + n // 4) * 4 + n % 4, fs, :]
            for c in range(cells):
                v = v + tab[1, c * 16 + n:c * 16 + n + 1] * t[c]
            store(n, fs, v)
        return carry

    lax.fori_loop(0, 8, back, 0)


def exchange_kernel(
    n_strip, n_band,
    state, wind_x, wind_y, jac, to_phys, to_dyn, mean, scale, w_in, w_hidden, w_out, bias_h, bias_o, counts,
    a_out, wi_out, wh_out, wo_out, bh_out, bo_out, tab_out, cnt_out, xt_out, inner_out,
    sbuf, wxv, wyv, jacv, coef, qbuf, edge_send, edge_recv, pack, pick, ysend, yrecv,
    jstrip, jband, jdiag, gather, halo, rmass, norm, partial, xt, tend, tp_s, td_s, cnt_s, rowv,
    in_sem, small_sem, w_sem, send_sem, recv_sem,
):
    s = lax.axis_index("strip")
    b = lax.axis_index("band")
    sp, sm = lax.rem(s + 1, n_strip), lax.rem(s + n_strip - 1, n_strip)
    bp, bm = lax.rem(b + 1, n_band), lax.rem(b + n_band - 1, n_band)

    barrier = pltpu.get_barrier_semaphore()
    for dev in ((sp, b), (sm, b), (s, bp), (s, bm), (sp, bp), (sp, bm), (sm, bp), (sm, bm)):
        pl.semaphore_signal(barrier, inc=1, device_id=dev, device_id_type=MESH)

    def local(src, dst, sem):
        c = pltpu.make_async_copy(src, dst, sem)
        c.start()
        return c

    small = [
        local(jac, jacv, small_sem.at[0]),
        local(wind_x, wxv, small_sem.at[1]),
        local(wind_y, wyv, small_sem.at[2]),
    ]

    def state_copy(n, x):
        return pltpu.make_async_copy(state.at[:, n, x, :], sbuf.at[n * 4 + x], in_sem.at[n * 4 + x])

    for x in range(2):
        for n in range(16):
            state_copy(n, x).start()

    copies = []

    def remote(src, dst, dev):
        n = len(copies)
        c = pltpu.make_async_remote_copy(
            src_ref=src, dst_ref=dst, send_sem=send_sem.at[n], recv_sem=recv_sem.at[n],
            device_id=dev, device_id_type=MESH,
        )
        copies.append(c)
        return c

    top, low = pl.ds(8, 8), pl.ds(0, 8)
    jac_band = [
        remote(jacv.at[:, top], jband.at[0], (s, bp)),
        remote(jacv.at[:, low], jband.at[1], (s, bm)),
    ]
    jac_strip = [
        remote(jacv.at[3], jstrip.at[0], (sp, b)),
        remote(jacv.at[0], jstrip.at[1], (sm, b)),
        remote(jacv.at[3, top], jdiag.at[0], (sp, bp)),
        remote(jacv.at[3, low], jdiag.at[1], (sp, bm)),
        remote(jacv.at[0, top], jdiag.at[2], (sm, bp)),
        remote(jacv.at[0, low], jdiag.at[3], (sm, bm)),
    ]
    edge_copies = [
        remote(edge_send.at[0], edge_recv.at[0], (sp, b)),
        remote(edge_send.at[1], edge_recv.at[1], (sm, b)),
    ]
    y_band = [
        remote(ysend, yrecv.at[0], (s, bp)),
        remote(ysend, yrecv.at[1], (s, bm)),
    ]
    y_diag = [
        remote(ysend, yrecv.at[2], (sp, bp)),
        remote(ysend, yrecv.at[3], (sp, bm)),
        remote(ysend, yrecv.at[4], (sm, bp)),
        remote(ysend, yrecv.at[5], (sm, bm)),
    ]

    wide = (32, 2048)
    row, col = (lax.broadcasted_iota(jnp.int32, wide, d) for d in (0, 1))
    at = (row // 2) * 128 + jnp.where(lax.rem(row, 2) == 0, 127, 0)
    pick[...] = jnp.where(col == at, F32(1.0), F32(0.0)).astype(BF16)

    for c in small:
        c.wait()
    for i in range(4):
        for jp in range(2):
            at = slice(i * 16 + jp * 8, i * 16 + jp * 8 + 8)
            first = lax.broadcasted_iota(jnp.int32, (8, 128), 0) < 4
            j0, j1 = 2 * jp, 2 * jp + 1
            m = jacv[i, jp * 8:jp * 8 + 8] * jnp.where(first, F32(QUAD[i, j0]), F32(QUAD[i, j1]))
            coef[0, at] = m
            coef[1, at] = m * wxv[at] * F32(-step_size * LEAD[i])
            lead = jnp.where(first, F32(-step_size * LEAD[j0]), F32(-step_size * LEAD[j1]))
            coef[2, at] = m * wyv[at] * lead

    lane8 = lanes(8)

    def advect_column(x):
        for n in range(16):
            state_copy(n, x).wait()

        def advect(k, carry):
            fs = pl.ds(pl.multiple_of(k * 8, 8), 8)
            v = [[sbuf[i * 16 + j * 4 + x, fs, :] for j in range(4)] for i in range(4)]
            q = [[None] * 4 for _ in range(4)]
            for j in range(4):
                d = mirrored(*[v[i][j] for i in range(4)])
                for i in range(4):
                    r = i * 16 + j * 4 + x
                    q[i][j] = coef[0, r:r + 1] * v[i][j] + coef[1, r:r + 1] * d[i]
            for i in range(4):
                d = mirrored(*v[i])
                for j in range(4):
                    r = i * 16 + j * 4 + x
                    q[i][j] = q[i][j] + coef[2, r:r + 1] * d[j]
                    qbuf[r, fs, :] = q[i][j]
                n = i * 4 + x
                pack[fs, n * 128:n * 128 + 128] = jnp.where(lane8 == 127, q[i][3], q[i][0])
            if x < 2:
                state_copy(k, x + 2).start()
            return carry

        lax.fori_loop(0, 16, advect, 0)

    advect_column(0)
    for j in range(4):
        edge_send[1, j] = qbuf[j * 4].astype(BF16)
    advect_column(1)
    later = [
        local(to_phys, tp_s, small_sem.at[3]),
        local(to_dyn, td_s, small_sem.at[4]),
        local(counts, cnt_s, small_sem.at[5]),
        local(mean, rowv.at[0], small_sem.at[6]),
        local(scale, rowv.at[1], small_sem.at[7]),
        local(bias_h, bh_out, small_sem.at[8]),
        local(bias_o, bo_out, small_sem.at[9]),
    ]
    weights = [
        local(w_in, wi_out, w_sem.at[0]),
        local(w_hidden, wh_out, w_sem.at[1]),
        local(w_out, wo_out, w_sem.at[2]),
    ]
    advect_column(2)
    advect_column(3)
    for j in range(4):
        edge_send[0, j] = qbuf[48 + j * 4 + 3].astype(BF16)
    ysend[...] = lax.dot_general(
        pick[...], pack[...].astype(BF16), (((1,), (1,)), ((), ())), preferred_element_type=F32
    ).astype(BF16)
    pl.semaphore_wait(barrier, 8)
    for c in jac_band + y_band + edge_copies + y_diag + jac_strip:
        c.start()

    for c in later:
        c.wait()
    for c in range(4):
        for n in range(16):
            tab_out[0, pl.ds(c * 16 + n, 1)] = jnp.full((1, 128), tp_s[c, n], F32)
            tab_out[1, pl.ds(c * 16 + n, 1)] = jnp.full((1, 128), td_s[c, n], F32)
    norm[0] = jnp.broadcast_to(rowv[0:1], (128, 128)).T
    norm[1] = jnp.broadcast_to(rowv[1:2], (128, 128)).T
    cnt_out[...] = jnp.full((8, 128), cnt_s[b, s].astype(F32), F32)

    lane1 = lanes(1)

    def element(side, i, j, x):
        w = F32(QUAD[i, j])
        r = j * 4 + x
        if side is None:
            return coef[0, i * 16 + r:i * 16 + r + 1]
        r = r - 8 if side == 0 else r
        return w * jband[side, i, r:r + 1]

    def outer(strip_side, band_side, j):
        i, x = (3, 3) if strip_side == 0 else (0, 0)
        w = F32(QUAD[i, j])
        r = j * 4 + x
        if band_side is None:
            return w * jstrip[strip_side, r:r + 1]
        r = r - 8 if band_side == 0 else r
        return w * jdiag[strip_side * 2 + band_side, r:r + 1]

    def level_mass(level, side, j):
        if level == 0:
            return element(side, 0, j, 0) + outer(0, side, j)
        if level == 12:
            return element(side, 3, j, 3) + outer(1, side, j)
        x, i = divmod(level, 3)
        if i == 0:
            return element(side, 0, j, x) + element(side, 3, j, x - 1)
        return element(side, i, j, x)

    def masses_mid(levels):
        for level in levels:
            for j in (1, 2):
                rmass[pl.ds(level * 4 + j, 1)] = 1.0 / level_mass(level, None, j)

    def masses_rim(levels):
        for level in levels:
            m = {j: level_mass(level, None, j) for j in (0, 3)}
            before = jnp.where(lane1 == 127, level_mass(level, 0, 3), m[3])
            after = jnp.where(lane1 == 0, level_mass(level, 1, 0), m[0])
            rmass[pl.ds(level * 4, 1)] = 1.0 / (m[0] + pltpu.roll(before, 1, 1))
            rmass[pl.ds(level * 4 + 3, 1)] = 1.0 / (m[3] + pltpu.roll(after, 127, 1))

    odd = lax.rem(lax.broadcasted_iota(jnp.int32, (32, 128), 0), 2) == 1

    def sort_rows(t):
        from_left = pltpu.roll(yrecv[2 * t].astype(F32), 1, 0)
        from_right = pltpu.roll(yrecv[2 * t + 1].astype(F32), 31, 0)
        gather[t * 32:(t + 1) * 32] = jnp.where(odd, from_left, from_right)

    def pair(t, i, x):
        r = t * 32 + 2 * (i * 4 + x)
        return gather[r:r + 2]

    def level_rows(level):
        x, i = divmod(level, 3)
        if level == 0:
            return pair(0, 0, 0) + pair(1, 3, 3)
        if level == 12:
            return pair(0, 3, 3) + pair(2, 0, 0)
        if i == 0:
            return pair(0, 0, x) + pair(0, 3, x - 1)
        return pair(0, i, x)

    def halos(levels):
        halo[...] = jnp.zeros((128, 128), F32)
        for level in levels:
            halo[2 * level:2 * level + 2] = level_rows(level)
        halo[...] = halo[...].T

    lane16 = lanes(16)

    def strip_sum(level, j, fs):
        x, i = divmod(level, 3)
        if level == 12:
            return qbuf[48 + j * 4 + 3, fs, :] + edge_recv[1, j, fs, :].astype(F32)
        u = qbuf[i * 16 + j * 4 + x, fs, :]
        if level == 0:
            return u + edge_recv[0, j, fs, :].astype(F32)
        return u + qbuf[48 + j * 4 + x - 1, fs, :] if i == 0 else u

    def assemble_mid(level, fs):
        for j in (1, 2):
            p = level * 4 + j
            a_out[p, fs, :] = strip_sum(level, j, fs) * rmass[p:p + 1]

    def assemble_rim(level, fs, h):
        low, high = strip_sum(level, 0, fs), strip_sum(level, 3, fs)
        hr = pltpu.roll(h, 128 - (2 * level + 1), 1)
        first = low + jnp.where(lane16 == 0, hr, pltpu.roll(high, 1, 1))
        last = high + jnp.where(lane16 == 127, hr, pltpu.roll(low, 127, 1))
        p = level * 4
        a_out[p, fs, :] = first * rmass[p:p + 1]
        a_out[p + 3, fs, :] = last * rmass[p + 3:p + 4]

    def chunks(step):
        def run(k, carry):
            step(pl.ds(pl.multiple_of(k * 16, 16), 16))
            return carry

        lax.fori_loop(0, 8, run, 0)

    def point(p, fs):
        return a_out[p, fs, :]

    def normal(v, fs):
        return ((v - norm[0, fs, :]) * norm[1, fs, :]).astype(BF16)

    inner = range(1, 12)
    rows_of = {x: [(i, 3 * x + i) for i in range(4) if 3 * x + i in inner] for x in range(4)}

    masses_mid(inner)

    def mid(fs):
        for level in inner:
            assemble_mid(level, fs)

    chunks(mid)
    for x in range(4):
        def mid_columns(fs, x=x):
            acc = columns_part(point, tab_out, rows_of[x], (1, 2), fs, [None] * 4)
            for c in range(4):
                partial[x, c, fs, :] = acc[c]

        chunks(mid_columns)

    for c in jac_band:
        c.wait_recv()
    masses_rim(inner)
    for c in y_band:
        c.wait_recv()
    sort_rows(0)
    halos(inner)

    def rim(fs):
        h = halo[fs, :]
        for level in inner:
            assemble_rim(level, fs, h)

    chunks(rim)
    for x in (1, 2, 0, 3):
        def rim_columns(fs, x=x):
            acc = [partial[x, c, fs, :] for c in range(4)]
            acc = columns_part(point, tab_out, rows_of[x], (0, 3), fs, acc)
            for c in range(4):
                if x in (1, 2):
                    at = c * 256 + (x - 1) * 128
                    xt[fs, at:at + 128] = normal(acc[c], fs)
                else:
                    partial[x, c, fs, :] = acc[c]

        chunks(rim_columns)

    for c in weights:
        c.wait()
    network(xt, wi_out, wh_out, wo_out, bh_out, bo_out, cnt_out, tend, (1, 2), (0, 1))
    for g, x in enumerate((1, 2)):
        def store(n, fs, v, g=g):
            inner_out[g, n, fs, :] = v

        back_loop(a_out, tab_out, tend, g, x, 4, store)

    for c in jac_strip + y_diag + edge_copies:
        c.wait_recv()
    masses_mid((0, 12))
    masses_rim((0, 12))
    sort_rows(1)
    sort_rows(2)
    halos((0, 12))

    def assemble_outer(fs):
        h = halo[fs, :]
        for g, (level, i) in enumerate(((0, 0), (12, 3))):
            assemble_mid(level, fs)
            assemble_rim(level, fs, h)
            acc = [partial[3 * g, c, fs, :] for c in range(4)]
            acc = columns_part(point, tab_out, [(i, level)], range(4), fs, acc)
            for c in range(4):
                at = c * 256 + g * 128
                xt_out[fs, at:at + 128] = normal(acc[c], fs)

    chunks(assemble_outer)
    for c in copies:
        c.wait_send()


def physics_kernel(a, wi, wh, wo, bh, bo, tab, cnt, xt, inner, out, tend, obuf, out_sem):
    copies = []

    def send(src, n, x):
        c = pltpu.make_async_copy(src, out.at[:, n * 4 + x, :], out_sem.at[len(copies)])
        c.start()
        copies.append(c)

    for g, x in enumerate((1, 2)):
        for n in range(16):
            send(inner.at[g, n], n, x)
    sends = [
        [pltpu.make_async_copy(obuf.at[g, n], out.at[:, n * 4 + x, :], out_sem.at[32 + g * 16 + n]) for n in range(16)]
        for g, x in enumerate((0, 3))
    ]

    def rest(parts):
        network(xt, wi, wh, wo, bh, bo, cnt, tend, (0, 3), parts)
        for g, x in enumerate((0, 3)):
            def store(n, fs, v, g=g):
                obuf[g, n, fs, :] = v

            back_loop(a, tab, tend, g, x, 2 * len(parts), store)
            for c in sends[g]:
                c.start()

    many = jnp.max(cnt[...]) > F32(1024.0)

    @pl.when(many)
    def _():
        rest((0, 1))

    @pl.when(jnp.logical_not(many))
    def _():
        rest((0,))

    for group in sends:
        copies.extend(group)
    for c in copies:
        c.wait()


def body(
    state, wind_x, wind_y, jacobian, to_physics, to_dynamics, feature_mean, feature_scale,
    w_in, w_hidden, w_out, bias_hidden, bias_out, live_counts,
):
    n_strip, n_band = lax.axis_size("strip"), lax.axis_size("band")
    hbm = pl.BlockSpec(memory_space=pltpu.HBM)
    vmem = pl.BlockSpec(memory_space=pltpu.VMEM)
    args = (
        state.reshape(128, 16, 4, 128), wind_x.reshape(64, 128), wind_y.reshape(64, 128),
        jacobian.reshape(4, 16, 128), to_physics, to_dynamics.T, feature_mean, feature_scale,
        w_in, w_hidden, w_out, bias_hidden, bias_out.reshape(1, 128), live_counts.T,
    )
    args = [pltpu.with_memory_space_constraint(v, pltpu.HBM) for v in args]
    dma = pltpu.SemaphoreType.DMA
    made = pl.pallas_call(
        lambda *refs: exchange_kernel(n_strip, n_band, *refs),
        out_shape=[
            pltpu.VMEM((52, 128, 128), F32),
            pltpu.VMEM((128, 512), BF16),
            pltpu.VMEM((4, 512, 512), BF16),
            pltpu.VMEM((512, 128), BF16),
            pltpu.VMEM((5, 512), F32),
            pltpu.VMEM((1, 128), F32),
            pltpu.VMEM((2, 64, 128), F32),
            pltpu.VMEM((8, 128), F32),
            pltpu.VMEM((128, 1024), BF16),
            pltpu.VMEM((2, 16, 128, 128), F32),
        ],
        in_specs=[hbm] * len(args),
        out_specs=[vmem] * 10,
        scratch_shapes=[
            pltpu.VMEM((64, 128, 128), F32),
            pltpu.VMEM((64, 128), F32),
            pltpu.VMEM((64, 128), F32),
            pltpu.VMEM((4, 16, 128), F32),
            pltpu.VMEM((3, 64, 128), F32),
            pltpu.VMEM((64, 128, 128), F32),
            pltpu.VMEM((2, 4, 128, 128), BF16),
            pltpu.VMEM((2, 4, 128, 128), BF16),
            pltpu.VMEM((128, 2048), F32),
            pltpu.VMEM((32, 2048), BF16),
            pltpu.VMEM((32, 128), BF16),
            pltpu.VMEM((6, 32, 128), BF16),
            pltpu.VMEM((2, 16, 128), F32),
            pltpu.VMEM((2, 4, 8, 128), F32),
            pltpu.VMEM((4, 8, 128), F32),
            pltpu.VMEM((96, 128), F32),
            pltpu.VMEM((128, 128), F32),
            pltpu.VMEM((52, 128), F32),
            pltpu.VMEM((2, 128, 128), F32),
            pltpu.VMEM((4, 4, 128, 128), F32),
            pltpu.VMEM((128, 1024), BF16),
            pltpu.VMEM((2, 4, 128, 128), F32),
            pltpu.SMEM((4, 16), F32),
            pltpu.SMEM((4, 16), F32),
            pltpu.SMEM((n_band, n_strip), jnp.int32),
            pltpu.VMEM((2, 128), F32),
            dma((64,)),
            dma((10,)),
            dma((3,)),
            dma((16,)),
            dma((16,)),
        ],
        name="exchange",
        compiler_params=pltpu.CompilerParams(
            collective_id=0, has_side_effects=True, vmem_limit_bytes=32 << 20
        ),
    )(*args)
    out = pl.pallas_call(
        physics_kernel,
        out_shape=jax.ShapeDtypeStruct((128, 64, 128), F32),
        in_specs=[vmem] * 10,
        out_specs=hbm,
        scratch_shapes=[
            pltpu.VMEM((2, 4, 128, 128), F32),
            pltpu.VMEM((2, 16, 128, 128), F32),
            dma((64,)),
        ],
        name="physics",
        compiler_params=pltpu.CompilerParams(vmem_limit_bytes=28 << 20),
    )(*made)
    return out.reshape(state.shape)


def solution(mesh):
    placed = (
        P(None, None, None, "strip", "band"),
        P(None, None, "strip", "band"),
        P(None, None, "strip", "band"),
        P(None, None, "strip", "band"),
        P(), P(), P(), P(), P(), P(), P(), P(), P(), P(),
    )
    return jax.shard_map(
        body,
        mesh=mesh,
        in_specs=placed,
        out_specs=P(None, None, None, "strip", "band"),
        check_vma=False,
    )
```

```python
import jax
import jax.numpy as jnp
import numpy as np
from jax import lax
from jax.experimental import pallas as pl
from jax.experimental.pallas import tpu as pltpu
from jax.sharding import PartitionSpec as P

MESH = pl.DeviceIdType.MESH
step_size = 0.1
slope = 0.15
F32 = jnp.float32
BF16 = jnp.bfloat16


def gll_tables():
    nodes = np.array([-1.0, -1.0 / np.sqrt(5.0), 1.0 / np.sqrt(5.0), 1.0])
    weights = np.array([1.0 / 6.0, 5.0 / 6.0, 5.0 / 6.0, 1.0 / 6.0])
    derivative = np.zeros((4, 4))
    for first in range(4):
        for second in range(4):
            if first != second:
                top = np.prod([nodes[first] - nodes[other] for other in range(4) if other != first])
                bottom = np.prod(
                    [nodes[second] - nodes[other] for other in range(4) if other != second]
                )
                derivative[first, second] = top / (bottom * (nodes[first] - nodes[second]))
            else:
                derivative[first, first] = np.sum(
                    [1.0 / (nodes[first] - nodes[other]) for other in range(4) if other != first]
                )
    return (weights, derivative)


WEIGHTS, DERIV = gll_tables()
QUAD = np.outer(WEIGHTS, WEIGHTS)
EVEN = [(DERIV[r, 0] + DERIV[r, 3]) / 2 for r in (0, 1)]
ODD0 = [(DERIV[r, 0] - DERIV[r, 3]) / 2 for r in (0, 1)]
ODD1 = [(DERIV[r, 1] - DERIV[r, 2]) / 2 for r in (0, 1)]
LEAD = [ODD0[0], ODD1[1], ODD1[1], ODD0[0]]


def mirrored(s0, s1, s2, s3):
    even = (s0 + s3) - (s1 + s2)
    far, near = s0 - s3, s1 - s2
    outer = far + F32(ODD1[0] / ODD0[0]) * near
    inner = near + F32(ODD0[1] / ODD1[1]) * far
    outer_e = F32(EVEN[0] / ODD0[0]) * even
    inner_e = F32(EVEN[1] / ODD1[1]) * even
    return outer + outer_e, inner + inner_e, inner - inner_e, outer - outer_e


def lanes(rows):
    return lax.broadcasted_iota(jnp.int32, (rows, 128), 1)


def columns_part(a_of, tab, levels, nodes, fs, acc):
    for i, level in levels:
        for j in nodes:
            v = a_of(level * 4 + j, fs)
            for c in range(4):
                r = c * 16 + i * 4 + j
                term = tab[0, r:r + 1] * v
                acc[c] = term if acc[c] is None else acc[c] + term
    return acc


def network(xt, wi, wh, wo, bh, bo, cnt, tend, xs, parts):
    lane = lanes(1).astype(F32)

    def act(acc, bias):
        v = acc + bias
        return jnp.maximum(v, F32(slope) * v).astype(BF16)

    def dot(p, q):
        return jnp.dot(p, q, preferred_element_type=F32)

    hs = [act(dot(xt[:, p[0] * 256:(p[-1] + 1) * 256].T, wi[...]), bh[0:1]) for p in parts]
    for layer in range(4):
        hs = [act(dot(h, wh[layer]), bh[layer + 1:layer + 2]) for h in hs]
    for p, h in zip(parts, hs):
        raw = (dot(h, wo[...]) + bo[...]).astype(BF16).T
        for c in p:
            for g in range(2):
                live = lane + F32(c * 512 + xs[g] * 128) < cnt[0:1]
                at = ((c - p[0]) * 2 + g) * 128
                tend[g, c] = jnp.where(live, raw[:, at:at + 128].astype(F32), F32(0.0))


def back_loop(a, tab, tend, g, x, cells, store):
    def back(k, carry):
        fs = pl.ds(pl.multiple_of(k * 16, 16), 16)
        t = [tend[g, c, fs, :] for c in range(cells)]
        for n in range(16):
            v = a[(3 * x + n // 4) * 4 + n % 4, fs, :]
            for c in range(cells):
                v = v + tab[1, c * 16 + n:c * 16 + n + 1] * t[c]
            store(n, fs, v)
        return carry

    lax.fori_loop(0, 8, back, 0)


def exchange_kernel(
    n_strip, n_band,
    state, wind_x, wind_y, jac, to_phys, to_dyn, mean, scale, w_in, w_hidden, w_out, bias_h, bias_o, counts,
    a_out, wi_out, wh_out, wo_out, bh_out, bo_out, tab_out, cnt_out, xt_out, inner_out,
    sbuf, wxv, wyv, jacv, coef, qbuf, edge_send, edge_recv, pack, pick, ysend, yrecv,
    jstrip, jband, jdiag, gather, halo, rmass, norm, partial, xt, tend, tp_s, td_s, cnt_s, rowv,
    in_sem, small_sem, w_sem, send_sem, recv_sem,
):
    s = lax.axis_index("strip")
    b = lax.axis_index("band")
    sp, sm = lax.rem(s + 1, n_strip), lax.rem(s + n_strip - 1, n_strip)
    bp, bm = lax.rem(b + 1, n_band), lax.rem(b + n_band - 1, n_band)

    def state_copy(n, x):
        return pltpu.make_async_copy(state.at[:, n, x, :], sbuf.at[n * 4 + x], in_sem.at[n * 4 + x])

    def local(src, dst, sem, priority=0):
        c = pltpu.make_async_copy(src, dst, sem)
        c.start(priority=priority)
        return c

    small = [
        local(jac, jacv, small_sem.at[0]),
        local(wind_x, wxv, small_sem.at[1]),
        local(wind_y, wyv, small_sem.at[2]),
    ]
    for n in range(16):
        state_copy(n, 0).start()
    barrier = pltpu.get_barrier_semaphore()
    for dev in ((sp, b), (sm, b), (s, bp), (s, bm), (sp, bp), (sp, bm), (sm, bp), (sm, bm)):
        pl.semaphore_signal(barrier, inc=1, device_id=dev, device_id_type=MESH)
    for x in range(1, 4):
        for n in range(16):
            state_copy(n, x).start(priority=1)

    copies = []

    def remote(src, dst, dev):
        n = len(copies)
        c = pltpu.make_async_remote_copy(
            src_ref=src, dst_ref=dst, send_sem=send_sem.at[n], recv_sem=recv_sem.at[n],
            device_id=dev, device_id_type=MESH,
        )
        copies.append(c)
        return c

    top, low = pl.ds(8, 8), pl.ds(0, 8)
    jac_band = [
        remote(jacv.at[:, top], jband.at[0], (s, bp)),
        remote(jacv.at[:, low], jband.at[1], (s, bm)),
    ]
    jac_strip = [
        remote(jacv.at[3], jstrip.at[0], (sp, b)),
        remote(jacv.at[0], jstrip.at[1], (sm, b)),
        remote(jacv.at[3, top], jdiag.at[0], (sp, bp)),
        remote(jacv.at[3, low], jdiag.at[1], (sp, bm)),
        remote(jacv.at[0, top], jdiag.at[2], (sm, bp)),
        remote(jacv.at[0, low], jdiag.at[3], (sm, bm)),
    ]
    edge_copies = [
        remote(edge_send.at[0], edge_recv.at[0], (sp, b)),
        remote(edge_send.at[1], edge_recv.at[1], (sm, b)),
    ]
    y_band = [
        remote(ysend, yrecv.at[0], (s, bp)),
        remote(ysend, yrecv.at[1], (s, bm)),
    ]
    y_diag = [
        remote(ysend, yrecv.at[2], (sp, bp)),
        remote(ysend, yrecv.at[3], (sp, bm)),
        remote(ysend, yrecv.at[4], (sm, bp)),
        remote(ysend, yrecv.at[5], (sm, bm)),
    ]

    wide = (32, 2048)
    row, col = (lax.broadcasted_iota(jnp.int32, wide, d) for d in (0, 1))
    at = (row // 2) * 128 + jnp.where(lax.rem(row, 2) == 0, 127, 0)
    pick[...] = jnp.where(col == at, F32(1.0), F32(0.0)).astype(BF16)

    for c in small:
        c.wait()
    for i in range(4):
        for jp in range(2):
            at = slice(i * 16 + jp * 8, i * 16 + jp * 8 + 8)
            first = lax.broadcasted_iota(jnp.int32, (8, 128), 0) < 4
            j0, j1 = 2 * jp, 2 * jp + 1
            m = jacv[i, jp * 8:jp * 8 + 8] * jnp.where(first, F32(QUAD[i, j0]), F32(QUAD[i, j1]))
            coef[0, at] = m
            coef[1, at] = m * wxv[at] * F32(-step_size * LEAD[i])
            lead = jnp.where(first, F32(-step_size * LEAD[j0]), F32(-step_size * LEAD[j1]))
            coef[2, at] = m * wyv[at] * lead

    lane8 = lanes(8)

    def advect_column(x):
        for n in range(16):
            state_copy(n, x).wait()

        def advect(k, carry):
            fs = pl.ds(pl.multiple_of(k * 8, 8), 8)
            v = [[sbuf[i * 16 + j * 4 + x, fs, :] for j in range(4)] for i in range(4)]
            q = [[None] * 4 for _ in range(4)]
            for j in range(4):
                d = mirrored(*[v[i][j] for i in range(4)])
                for i in range(4):
                    r = i * 16 + j * 4 + x
                    q[i][j] = coef[0, r:r + 1] * v[i][j] + coef[1, r:r + 1] * d[i]
            for i in range(4):
                d = mirrored(*v[i])
                for j in range(4):
                    r = i * 16 + j * 4 + x
                    q[i][j] = q[i][j] + coef[2, r:r + 1] * d[j]
                    qbuf[r, fs, :] = q[i][j]
                n = i * 4 + x
                pack[fs, n * 128:n * 128 + 128] = jnp.where(lane8 == 127, q[i][3], q[i][0])
            return carry

        lax.fori_loop(0, 16, advect, 0)

    advect_column(0)
    for j in range(4):
        edge_send[1, j] = qbuf[j * 4].astype(BF16)
    advect_column(1)
    later = [
        local(to_phys, tp_s, small_sem.at[3]),
        local(to_dyn, td_s, small_sem.at[4]),
        local(counts, cnt_s, small_sem.at[5]),
        local(mean, rowv.at[0], small_sem.at[6]),
        local(scale, rowv.at[1], small_sem.at[7]),
        local(bias_h, bh_out, small_sem.at[8]),
        local(bias_o, bo_out, small_sem.at[9]),
    ]
    weights = [
        local(w_in, wi_out, w_sem.at[0], 1),
        local(w_hidden, wh_out, w_sem.at[1], 1),
        local(w_out, wo_out, w_sem.at[2], 1),
    ]
    advect_column(2)
    advect_column(3)
    for j in range(4):
        edge_send[0, j] = qbuf[48 + j * 4 + 3].astype(BF16)
    ysend[...] = lax.dot_general(
        pick[...], pack[...].astype(BF16), (((1,), (1,)), ((), ())), preferred_element_type=F32
    ).astype(BF16)
    pl.semaphore_wait(barrier, 8)
    for c in y_band + jac_band + y_diag + jac_strip + edge_copies:
        c.start()

    for c in later:
        c.wait()
    for c in range(4):
        for n in range(16):
            tab_out[0, pl.ds(c * 16 + n, 1)] = jnp.full((1, 128), tp_s[c, n], F32)
            tab_out[1, pl.ds(c * 16 + n, 1)] = jnp.full((1, 128), td_s[c, n], F32)
    norm[0] = jnp.broadcast_to(rowv[0:1], (128, 128)).T
    norm[1] = jnp.broadcast_to(rowv[1:2], (128, 128)).T
    cnt_out[...] = jnp.full((8, 128), cnt_s[b, s].astype(F32), F32)

    lane1 = lanes(1)

    def element(side, i, j, x):
        w = F32(QUAD[i, j])
        r = j * 4 + x
        if side is None:
            return coef[0, i * 16 + r:i * 16 + r + 1]
        r = r - 8 if side == 0 else r
        return w * jband[side, i, r:r + 1]

    def outer(strip_side, band_side, j):
        i, x = (3, 3) if strip_side == 0 else (0, 0)
        w = F32(QUAD[i, j])
        r = j * 4 + x
        if band_side is None:
            return w * jstrip[strip_side, r:r + 1]
        r = r - 8 if band_side == 0 else r
        return w * jdiag[strip_side * 2 + band_side, r:r + 1]

    def level_mass(level, side, j):
        if level == 0:
            return element(side, 0, j, 0) + outer(0, side, j)
        if level == 12:
            return element(side, 3, j, 3) + outer(1, side, j)
        x, i = divmod(level, 3)
        if i == 0:
            return element(side, 0, j, x) + element(side, 3, j, x - 1)
        return element(side, i, j, x)

    def masses_mid(levels):
        for level in levels:
            for j in (1, 2):
                rmass[pl.ds(level * 4 + j, 1)] = 1.0 / level_mass(level, None, j)

    def masses_rim(levels):
        for level in levels:
            m = {j: level_mass(level, None, j) for j in (0, 3)}
            before = jnp.where(lane1 == 127, level_mass(level, 0, 3), m[3])
            after = jnp.where(lane1 == 0, level_mass(level, 1, 0), m[0])
            rmass[pl.ds(level * 4, 1)] = 1.0 / (m[0] + pltpu.roll(before, 1, 1))
            rmass[pl.ds(level * 4 + 3, 1)] = 1.0 / (m[3] + pltpu.roll(after, 127, 1))

    odd = lax.rem(lax.broadcasted_iota(jnp.int32, (32, 128), 0), 2) == 1

    def sort_rows(t):
        from_left = pltpu.roll(yrecv[2 * t].astype(F32), 1, 0)
        from_right = pltpu.roll(yrecv[2 * t + 1].astype(F32), 31, 0)
        gather[t * 32:(t + 1) * 32] = jnp.where(odd, from_left, from_right)

    def pair(t, i, x):
        r = t * 32 + 2 * (i * 4 + x)
        return gather[r:r + 2]

    def level_rows(level):
        x, i = divmod(level, 3)
        if level == 0:
            return pair(0, 0, 0) + pair(1, 3, 3)
        if level == 12:
            return pair(0, 3, 3) + pair(2, 0, 0)
        if i == 0:
            return pair(0, 0, x) + pair(0, 3, x - 1)
        return pair(0, i, x)

    def halos(levels):
        halo[...] = jnp.zeros((128, 128), F32)
        for level in levels:
            halo[2 * level:2 * level + 2] = level_rows(level)
        halo[...] = halo[...].T

    lane16 = lanes(16)

    def strip_sum(level, j, fs):
        x, i = divmod(level, 3)
        if level == 12:
            return qbuf[48 + j * 4 + 3, fs, :] + edge_recv[1, j, fs, :].astype(F32)
        u = qbuf[i * 16 + j * 4 + x, fs, :]
        if level == 0:
            return u + edge_recv[0, j, fs, :].astype(F32)
        return u + qbuf[48 + j * 4 + x - 1, fs, :] if i == 0 else u

    def assemble_mid(level, fs):
        for j in (1, 2):
            p = level * 4 + j
            a_out[p, fs, :] = strip_sum(level, j, fs) * rmass[p:p + 1]

    def assemble_rim(level, fs, h):
        low, high = strip_sum(level, 0, fs), strip_sum(level, 3, fs)
        hr = pltpu.roll(h, 128 - (2 * level + 1), 1)
        first = low + jnp.where(lane16 == 0, hr, pltpu.roll(high, 1, 1))
        last = high + jnp.where(lane16 == 127, hr, pltpu.roll(low, 127, 1))
        p = level * 4
        a_out[p, fs, :] = first * rmass[p:p + 1]
        a_out[p + 3, fs, :] = last * rmass[p + 3:p + 4]

    def chunks(step):
        def run(k, carry):
            step(pl.ds(pl.multiple_of(k * 16, 16), 16))
            return carry

        lax.fori_loop(0, 8, run, 0)

    def point(p, fs):
        return a_out[p, fs, :]

    def normal(v, fs):
        return ((v - norm[0, fs, :]) * norm[1, fs, :]).astype(BF16)

    inner = range(1, 12)
    rows_of = {x: [(i, 3 * x + i) for i in range(4) if 3 * x + i in inner] for x in range(4)}

    masses_mid(inner)

    def mid(fs):
        for level in inner:
            assemble_mid(level, fs)

    chunks(mid)
    for x in range(4):
        def mid_columns(fs, x=x):
            acc = columns_part(point, tab_out, rows_of[x], (1, 2), fs, [None] * 4)
            for c in range(4):
                partial[x, c, fs, :] = acc[c]

        chunks(mid_columns)

    for c in jac_band:
        c.wait_recv()
    masses_rim(inner)
    for c in y_band:
        c.wait_recv()
    sort_rows(0)
    halos(inner)

    def rim(fs):
        h = halo[fs, :]
        for level in inner:
            assemble_rim(level, fs, h)

    chunks(rim)
    for x in (1, 2, 0, 3):
        def rim_columns(fs, x=x):
            acc = [partial[x, c, fs, :] for c in range(4)]
            acc = columns_part(point, tab_out, rows_of[x], (0, 3), fs, acc)
            for c in range(4):
                if x in (1, 2):
                    at = c * 256 + (x - 1) * 128
                    xt[fs, at:at + 128] = normal(acc[c], fs)
                else:
                    partial[x, c, fs, :] = acc[c]

        chunks(rim_columns)

    for c in weights:
        c.wait()
    network(xt, wi_out, wh_out, wo_out, bh_out, bo_out, cnt_out, tend, (1, 2), ((0, 1), (2, 3)))
    for g, x in enumerate((1, 2)):
        def store(n, fs, v, g=g):
            inner_out[g, n, fs, :] = v

        back_loop(a_out, tab_out, tend, g, x, 4, store)

    for c in jac_strip:
        c.wait_recv()
    masses_mid((0, 12))
    masses_rim((0, 12))
    for c in y_diag:
        c.wait_recv()
    sort_rows(1)
    sort_rows(2)
    halos((0, 12))
    for c in edge_copies:
        c.wait_recv()

    def assemble_outer(fs):
        h = halo[fs, :]
        for g, (level, i) in enumerate(((0, 0), (12, 3))):
            assemble_mid(level, fs)
            assemble_rim(level, fs, h)
            acc = [partial[3 * g, c, fs, :] for c in range(4)]
            acc = columns_part(point, tab_out, [(i, level)], range(4), fs, acc)
            for c in range(4):
                at = c * 256 + g * 128
                xt_out[fs, at:at + 128] = normal(acc[c], fs)

    chunks(assemble_outer)
    for c in copies:
        c.wait_send()


def physics_kernel(a, wi, wh, wo, bh, bo, tab, cnt, xt, inner, out, tend, obuf, out_sem):
    copies = []

    def send(src, n, x):
        c = pltpu.make_async_copy(src, out.at[:, n, x, :], out_sem.at[len(copies)])
        c.start(priority=1)
        copies.append(c)

    for g, x in enumerate((1, 2)):
        for n in range(16):
            send(inner.at[g, n], n, x)
    def row_copy(g, n):
        return pltpu.make_async_copy(obuf.at[g, n], out.at[:, n, 3 * g, :], out_sem.at[32 + g * 16 + n])

    def rest(parts):
        network(xt, wi, wh, wo, bh, bo, cnt, tend, (0, 3), parts)
        cells = sum(parts, ())
        for g in range(2):
            def back(n, carry):
                for h in range(2):
                    fs = pl.ds(h * 64, 64)
                    v = a[g * 36 + n, fs, :]
                    for c in cells:
                        v = v + tab[1, pl.ds(c * 16 + n, 1)] * tend[g, c, fs, :]
                    obuf[g, n, fs, :] = v
                row_copy(g, n).start()
                return carry

            lax.fori_loop(0, 16, back, 0)

    many = jnp.max(cnt[...]) > F32(1024.0)

    @pl.when(many)
    def _():
        rest(((0, 1), (2, 3)))

    @pl.when(jnp.logical_not(many))
    def _():
        rest(((0,), (1,)))

    copies.extend(row_copy(g, n) for g in range(2) for n in range(16))
    for c in copies:
        c.wait()


def body(
    state, wind_x, wind_y, jacobian, to_physics, to_dynamics, feature_mean, feature_scale,
    w_in, w_hidden, w_out, bias_hidden, bias_out, live_counts,
):
    n_strip, n_band = lax.axis_size("strip"), lax.axis_size("band")
    hbm = pl.BlockSpec(memory_space=pltpu.HBM)
    vmem = pl.BlockSpec(memory_space=pltpu.VMEM)
    args = (
        state.reshape(128, 16, 4, 128), wind_x.reshape(64, 128), wind_y.reshape(64, 128),
        jacobian.reshape(4, 16, 128), to_physics, to_dynamics.T, feature_mean, feature_scale,
        w_in, w_hidden, w_out, bias_hidden, bias_out.reshape(1, 128), live_counts.T,
    )
    args = [pltpu.with_memory_space_constraint(v, pltpu.HBM) for v in args]
    dma = pltpu.SemaphoreType.DMA
    made = pl.pallas_call(
        lambda *refs: exchange_kernel(n_strip, n_band, *refs),
        out_shape=[
            pltpu.VMEM((52, 128, 128), F32),
            pltpu.VMEM((128, 512), BF16),
            pltpu.VMEM((4, 512, 512), BF16),
            pltpu.VMEM((512, 128), BF16),
            pltpu.VMEM((5, 512), F32),
            pltpu.VMEM((1, 128), F32),
            pltpu.VMEM((2, 64, 128), F32),
            pltpu.VMEM((8, 128), F32),
            pltpu.VMEM((128, 1024), BF16),
            pltpu.VMEM((2, 16, 128, 128), F32),
        ],
        in_specs=[hbm] * len(args),
        out_specs=[vmem] * 10,
        scratch_shapes=[
            pltpu.VMEM((64, 128, 128), F32),
            pltpu.VMEM((64, 128), F32),
            pltpu.VMEM((64, 128), F32),
            pltpu.VMEM((4, 16, 128), F32),
            pltpu.VMEM((3, 64, 128), F32),
            pltpu.VMEM((64, 128, 128), F32),
            pltpu.VMEM((2, 4, 128, 128), BF16),
            pltpu.VMEM((2, 4, 128, 128), BF16),
            pltpu.VMEM((128, 2048), F32),
            pltpu.VMEM((32, 2048), BF16),
            pltpu.VMEM((32, 128), BF16),
            pltpu.VMEM((6, 32, 128), BF16),
            pltpu.VMEM((2, 16, 128), F32),
            pltpu.VMEM((2, 4, 8, 128), F32),
            pltpu.VMEM((4, 8, 128), F32),
            pltpu.VMEM((96, 128), F32),
            pltpu.VMEM((128, 128), F32),
            pltpu.VMEM((52, 128), F32),
            pltpu.VMEM((2, 128, 128), F32),
            pltpu.VMEM((4, 4, 128, 128), F32),
            pltpu.VMEM((128, 1024), BF16),
            pltpu.VMEM((2, 4, 128, 128), F32),
            pltpu.SMEM((4, 16), F32),
            pltpu.SMEM((4, 16), F32),
            pltpu.SMEM((n_band, n_strip), jnp.int32),
            pltpu.VMEM((2, 128), F32),
            dma((64,)),
            dma((10,)),
            dma((3,)),
            dma((16,)),
            dma((16,)),
        ],
        name="exchange",
        compiler_params=pltpu.CompilerParams(
            collective_id=0, has_side_effects=True, vmem_limit_bytes=32 << 20
        ),
    )(*args)
    out = pl.pallas_call(
        physics_kernel,
        out_shape=jax.ShapeDtypeStruct((128, 16, 4, 128), F32),
        in_specs=[vmem] * 10,
        out_specs=hbm,
        scratch_shapes=[
            pltpu.VMEM((2, 4, 128, 128), F32),
            pltpu.VMEM((2, 16, 128, 128), F32),
            dma((64,)),
        ],
        name="physics",
        compiler_params=pltpu.CompilerParams(vmem_limit_bytes=28 << 20),
    )(*made)
    return out.reshape(state.shape)


def solution(mesh):
    placed = (
        P(None, None, None, "strip", "band"),
        P(None, None, "strip", "band"),
        P(None, None, "strip", "band"),
        P(None, None, "strip", "band"),
        P(), P(), P(), P(), P(), P(), P(), P(), P(), P(),
    )
    return jax.shard_map(
        body,
        mesh=mesh,
        in_specs=placed,
        out_specs=P(None, None, None, "strip", "band"),
        check_vma=False,
    )
```

```python
import jax
import jax.numpy as jnp
import numpy as np
from jax import lax
from jax.experimental import pallas as pl
from jax.experimental.pallas import tpu as pltpu
from jax.sharding import PartitionSpec as P

MESH = pl.DeviceIdType.MESH
step_size = 0.1
slope = 0.15
F32 = jnp.float32
BF16 = jnp.bfloat16


def gll_tables():
    nodes = np.array([-1.0, -1.0 / np.sqrt(5.0), 1.0 / np.sqrt(5.0), 1.0])
    weights = np.array([1.0 / 6.0, 5.0 / 6.0, 5.0 / 6.0, 1.0 / 6.0])
    derivative = np.zeros((4, 4))
    for first in range(4):
        for second in range(4):
            if first != second:
                top = np.prod([nodes[first] - nodes[other] for other in range(4) if other != first])
                bottom = np.prod(
                    [nodes[second] - nodes[other] for other in range(4) if other != second]
                )
                derivative[first, second] = top / (bottom * (nodes[first] - nodes[second]))
            else:
                derivative[first, first] = np.sum(
                    [1.0 / (nodes[first] - nodes[other]) for other in range(4) if other != first]
                )
    return (weights, derivative)


WEIGHTS, DERIV = gll_tables()
QUAD = np.outer(WEIGHTS, WEIGHTS)
EVEN = [(DERIV[r, 0] + DERIV[r, 3]) / 2 for r in (0, 1)]
ODD0 = [(DERIV[r, 0] - DERIV[r, 3]) / 2 for r in (0, 1)]
ODD1 = [(DERIV[r, 1] - DERIV[r, 2]) / 2 for r in (0, 1)]
LEAD = [ODD0[0], ODD1[1], ODD1[1], ODD0[0]]


def mirrored(s0, s1, s2, s3):
    even = (s0 + s3) - (s1 + s2)
    far, near = s0 - s3, s1 - s2
    outer = far + F32(ODD1[0] / ODD0[0]) * near
    inner = near + F32(ODD0[1] / ODD1[1]) * far
    outer_e = F32(EVEN[0] / ODD0[0]) * even
    inner_e = F32(EVEN[1] / ODD1[1]) * even
    return outer + outer_e, inner + inner_e, inner - inner_e, outer - outer_e


def lanes(rows):
    return lax.broadcasted_iota(jnp.int32, (rows, 128), 1)


def columns_part(a_of, tab, levels, nodes, fs, acc):
    for i, level in levels:
        for j in nodes:
            v = a_of(level * 4 + j, fs)
            for c in range(4):
                r = c * 16 + i * 4 + j
                term = tab[0, r:r + 1] * v
                acc[c] = term if acc[c] is None else acc[c] + term
    return acc


def network(xt, wi, wh, wo, bh, bo, cnt, tend, xs, parts):
    lane = lanes(1).astype(F32)

    def act(acc, bias):
        v = acc + bias
        return jnp.maximum(v, F32(slope) * v).astype(BF16)

    def dot(p, q):
        return jnp.dot(p, q, preferred_element_type=F32)

    hs = [act(dot(xt[:, p[0] * 256:(p[-1] + 1) * 256].T, wi[...]), bh[0:1]) for p in parts]
    for layer in range(4):
        hs = [act(dot(h, wh[layer]), bh[layer + 1:layer + 2]) for h in hs]
    for p, h in zip(parts, hs):
        raw = (dot(h, wo[...]) + bo[...]).astype(BF16).T
        for c in p:
            for g in range(2):
                live = lane + F32(c * 512 + xs[g] * 128) < cnt[0:1]
                at = ((c - p[0]) * 2 + g) * 128
                tend[g, c] = jnp.where(live, raw[:, at:at + 128].astype(F32), F32(0.0))


def back_loop(a, tab, tend, g, x, cells, store):
    def back(k, carry):
        fs = pl.ds(pl.multiple_of(k * 64, 64), 64)
        t = [tend[g, c, fs, :] for c in range(cells)]
        for n in range(16):
            v = a[(3 * x + n // 4) * 4 + n % 4, fs, :]
            for c in range(cells):
                v = v + tab[1, c * 16 + n:c * 16 + n + 1] * t[c]
            store(n, fs, v)
        return carry

    lax.fori_loop(0, 2, back, 0)


def exchange_kernel(
    n_strip, n_band,
    state, wind_x, wind_y, jac, to_phys, to_dyn, mean, scale, w_in, w_hidden, w_out, bias_h, bias_o, counts,
    a_out, wi_out, wh_out, wo_out, bh_out, bo_out, tab_out, cnt_out, xt_out, inner_out,
    sbuf, wxv, wyv, jacv, coef, qbuf, edge_send, edge_recv, pack, pick, ysend, yrecv,
    jstrip, jband, jdiag, gather, halo, rmass, norm, partial, xt, tend, tp_s, td_s, cnt_s, rowv,
    in_sem, small_sem, w_sem, send_sem, recv_sem,
):
    s = lax.axis_index("strip")
    b = lax.axis_index("band")
    sp, sm = lax.rem(s + 1, n_strip), lax.rem(s + n_strip - 1, n_strip)
    bp, bm = lax.rem(b + 1, n_band), lax.rem(b + n_band - 1, n_band)

    def state_copy(n, x):
        return pltpu.make_async_copy(state.at[:, n, x, :], sbuf.at[n * 4 + x], in_sem.at[n * 4 + x])

    def local(src, dst, sem, priority=0):
        c = pltpu.make_async_copy(src, dst, sem)
        c.start(priority=priority)
        return c

    small = [
        local(jac, jacv, small_sem.at[0]),
        local(wind_x, wxv, small_sem.at[1]),
        local(wind_y, wyv, small_sem.at[2]),
    ]
    for n in range(16):
        state_copy(n, 0).start()
    barrier = pltpu.get_barrier_semaphore()
    for dev in ((sp, b), (sm, b), (s, bp), (s, bm), (sp, bp), (sp, bm), (sm, bp), (sm, bm)):
        pl.semaphore_signal(barrier, inc=1, device_id=dev, device_id_type=MESH)
    for x in range(1, 4):
        for n in range(16):
            state_copy(n, x).start(priority=1)

    copies = []

    def remote(src, dst, dev):
        n = len(copies)
        c = pltpu.make_async_remote_copy(
            src_ref=src, dst_ref=dst, send_sem=send_sem.at[n], recv_sem=recv_sem.at[n],
            device_id=dev, device_id_type=MESH,
        )
        copies.append(c)
        return c

    top, low = pl.ds(8, 8), pl.ds(0, 8)
    jac_band = [
        remote(jacv.at[:, top], jband.at[0], (s, bp)),
        remote(jacv.at[:, low], jband.at[1], (s, bm)),
    ]
    jac_strip = [
        remote(jacv.at[3], jstrip.at[0], (sp, b)),
        remote(jacv.at[0], jstrip.at[1], (sm, b)),
        remote(jacv.at[3, top], jdiag.at[0], (sp, bp)),
        remote(jacv.at[3, low], jdiag.at[1], (sp, bm)),
        remote(jacv.at[0, top], jdiag.at[2], (sm, bp)),
        remote(jacv.at[0, low], jdiag.at[3], (sm, bm)),
    ]
    edge_copies = [
        remote(edge_send.at[0], edge_recv.at[0], (sp, b)),
        remote(edge_send.at[1], edge_recv.at[1], (sm, b)),
    ]
    y_band = [
        remote(ysend, yrecv.at[0], (s, bp)),
        remote(ysend, yrecv.at[1], (s, bm)),
    ]
    y_diag = [
        remote(ysend, yrecv.at[2], (sp, bp)),
        remote(ysend, yrecv.at[3], (sp, bm)),
        remote(ysend, yrecv.at[4], (sm, bp)),
        remote(ysend, yrecv.at[5], (sm, bm)),
    ]

    wide = (32, 2048)
    row, col = (lax.broadcasted_iota(jnp.int32, wide, d) for d in (0, 1))
    at = (row // 2) * 128 + jnp.where(lax.rem(row, 2) == 0, 127, 0)
    pick[...] = jnp.where(col == at, F32(1.0), F32(0.0)).astype(BF16)

    for c in small:
        c.wait()
    for i in range(4):
        for jp in range(2):
            at = slice(i * 16 + jp * 8, i * 16 + jp * 8 + 8)
            first = lax.broadcasted_iota(jnp.int32, (8, 128), 0) < 4
            j0, j1 = 2 * jp, 2 * jp + 1
            m = jacv[i, jp * 8:jp * 8 + 8] * jnp.where(first, F32(QUAD[i, j0]), F32(QUAD[i, j1]))
            coef[0, at] = m
            coef[1, at] = m * wxv[at] * F32(-step_size * LEAD[i])
            lead = jnp.where(first, F32(-step_size * LEAD[j0]), F32(-step_size * LEAD[j1]))
            coef[2, at] = m * wyv[at] * lead

    lane = lanes(16)

    def advect_column(x):
        for n in range(16):
            state_copy(n, x).wait()

        def advect(k, carry):
            fs = pl.ds(pl.multiple_of(k * 16, 16), 16)
            v = [[sbuf[i * 16 + j * 4 + x, fs, :] for j in range(4)] for i in range(4)]
            q = [[None] * 4 for _ in range(4)]
            for j in range(4):
                d = mirrored(*[v[i][j] for i in range(4)])
                for i in range(4):
                    r = i * 16 + j * 4 + x
                    q[i][j] = coef[0, r:r + 1] * v[i][j] + coef[1, r:r + 1] * d[i]
            for i in range(4):
                d = mirrored(*v[i])
                for j in range(4):
                    r = i * 16 + j * 4 + x
                    q[i][j] = q[i][j] + coef[2, r:r + 1] * d[j]
                    qbuf[r, fs, :] = q[i][j]
                n = i * 4 + x
                pack[fs, n * 128:n * 128 + 128] = jnp.where(lane == 127, q[i][3], q[i][0])
            return carry

        lax.fori_loop(0, 8, advect, 0)

    advect_column(0)
    for j in range(4):
        edge_send[1, j] = qbuf[j * 4].astype(BF16)
    advect_column(1)
    later = [
        local(to_phys, tp_s, small_sem.at[3]),
        local(to_dyn, td_s, small_sem.at[4]),
        local(counts, cnt_s, small_sem.at[5]),
        local(mean, rowv.at[0], small_sem.at[6]),
        local(scale, rowv.at[1], small_sem.at[7]),
        local(bias_h, bh_out, small_sem.at[8]),
        local(bias_o, bo_out, small_sem.at[9]),
    ]
    weights = [
        local(w_in, wi_out, w_sem.at[0], 1),
        local(w_hidden, wh_out, w_sem.at[1], 1),
        local(w_out, wo_out, w_sem.at[2], 1),
    ]
    advect_column(2)
    advect_column(3)
    for j in range(4):
        edge_send[0, j] = qbuf[48 + j * 4 + 3].astype(BF16)
    ysend[...] = lax.dot_general(
        pick[...], pack[...].astype(BF16), (((1,), (1,)), ((), ())), preferred_element_type=F32
    ).astype(BF16)
    pl.semaphore_wait(barrier, 8)
    for c in y_band + jac_band + y_diag + jac_strip + edge_copies:
        c.start()

    for c in later:
        c.wait()
    for c in range(4):
        for n in range(16):
            tab_out[0, pl.ds(c * 16 + n, 1)] = jnp.full((1, 128), tp_s[c, n], F32)
            tab_out[1, pl.ds(c * 16 + n, 1)] = jnp.full((1, 128), td_s[c, n], F32)
    norm[0] = jnp.broadcast_to(rowv[0:1], (128, 128)).T
    norm[1] = jnp.broadcast_to(rowv[1:2], (128, 128)).T
    cnt_out[...] = jnp.full((8, 128), cnt_s[b, s].astype(F32), F32)

    lane1 = lanes(1)

    def element(side, i, j, x):
        w = F32(QUAD[i, j])
        r = j * 4 + x
        if side is None:
            return coef[0, i * 16 + r:i * 16 + r + 1]
        r = r - 8 if side == 0 else r
        return w * jband[side, i, r:r + 1]

    def outer(strip_side, band_side, j):
        i, x = (3, 3) if strip_side == 0 else (0, 0)
        w = F32(QUAD[i, j])
        r = j * 4 + x
        if band_side is None:
            return w * jstrip[strip_side, r:r + 1]
        r = r - 8 if band_side == 0 else r
        return w * jdiag[strip_side * 2 + band_side, r:r + 1]

    def level_mass(level, side, j):
        if level == 0:
            return element(side, 0, j, 0) + outer(0, side, j)
        if level == 12:
            return element(side, 3, j, 3) + outer(1, side, j)
        x, i = divmod(level, 3)
        if i == 0:
            return element(side, 0, j, x) + element(side, 3, j, x - 1)
        return element(side, i, j, x)

    def masses_mid(levels):
        for level in levels:
            for j in (1, 2):
                rmass[pl.ds(level * 4 + j, 1)] = 1.0 / level_mass(level, None, j)

    def masses_rim(levels):
        for level in levels:
            m = {j: level_mass(level, None, j) for j in (0, 3)}
            before = jnp.where(lane1 == 127, level_mass(level, 0, 3), m[3])
            after = jnp.where(lane1 == 0, level_mass(level, 1, 0), m[0])
            rmass[pl.ds(level * 4, 1)] = 1.0 / (m[0] + pltpu.roll(before, 1, 1))
            rmass[pl.ds(level * 4 + 3, 1)] = 1.0 / (m[3] + pltpu.roll(after, 127, 1))

    odd = lax.rem(lax.broadcasted_iota(jnp.int32, (32, 128), 0), 2) == 1

    def sort_rows(t):
        from_left = pltpu.roll(yrecv[2 * t].astype(F32), 1, 0)
        from_right = pltpu.roll(yrecv[2 * t + 1].astype(F32), 31, 0)
        gather[t * 32:(t + 1) * 32] = jnp.where(odd, from_left, from_right)

    def pair(t, i, x):
        r = t * 32 + 2 * (i * 4 + x)
        return gather[r:r + 2]

    def level_rows(level):
        x, i = divmod(level, 3)
        if level == 0:
            return pair(0, 0, 0) + pair(1, 3, 3)
        if level == 12:
            return pair(0, 3, 3) + pair(2, 0, 0)
        if i == 0:
            return pair(0, 0, x) + pair(0, 3, x - 1)
        return pair(0, i, x)

    def halos(levels):
        halo[...] = jnp.zeros((128, 128), F32)
        for level in levels:
            halo[2 * level:2 * level + 2] = level_rows(level)
        halo[...] = halo[...].T

    def strip_sum(level, j, fs):
        x, i = divmod(level, 3)
        if level == 12:
            return qbuf[48 + j * 4 + 3, fs, :] + edge_recv[1, j, fs, :].astype(F32)
        u = qbuf[i * 16 + j * 4 + x, fs, :]
        if level == 0:
            return u + edge_recv[0, j, fs, :].astype(F32)
        return u + qbuf[48 + j * 4 + x - 1, fs, :] if i == 0 else u

    def assemble_mid(level, fs):
        made = {}
        for j in (1, 2):
            p = level * 4 + j
            made[p] = strip_sum(level, j, fs) * rmass[p:p + 1]
            a_out[p, fs, :] = made[p]
        return made

    def assemble_rim(level, fs, h):
        low, high = strip_sum(level, 0, fs), strip_sum(level, 3, fs)
        lane = lanes(low.shape[0])
        hr = pltpu.roll(h, 128 - (2 * level + 1), 1)
        first = low + jnp.where(lane == 0, hr, pltpu.roll(high, 1, 1))
        last = high + jnp.where(lane == 127, hr, pltpu.roll(low, 127, 1))
        p = level * 4
        made = {p: first * rmass[p:p + 1], p + 3: last * rmass[p + 3:p + 4]}
        a_out[p, fs, :] = made[p]
        a_out[p + 3, fs, :] = made[p + 3]
        return made

    def chunks(step, size):
        def run(k, carry):
            step(pl.ds(pl.multiple_of(k * size, size), size))
            return carry

        lax.fori_loop(0, 128 // size, run, 0)

    def point(p, fs):
        return a_out[p, fs, :]

    def normal(v, fs):
        return ((v - norm[0, fs, :]) * norm[1, fs, :]).astype(BF16)

    inner = range(1, 12)
    rows_of = {x: [(i, 3 * x + i) for i in range(4) if 3 * x + i in inner] for x in range(4)}

    masses_mid(inner)

    def mid(fs):
        for level in inner:
            assemble_mid(level, fs)

    chunks(mid, 64)
    for x in range(4):
        def mid_columns(fs, x=x):
            acc = columns_part(point, tab_out, rows_of[x], (1, 2), fs, [None] * 4)
            for c in range(4):
                partial[x, c, fs, :] = acc[c]

        chunks(mid_columns, 32)

    for c in jac_band:
        c.wait_recv()
    masses_rim(inner)
    for c in y_band:
        c.wait_recv()
    sort_rows(0)
    halos(inner)

    def rim(fs):
        h = halo[fs, :]
        for level in inner:
            assemble_rim(level, fs, h)

    chunks(rim, 64)
    for x in (1, 2, 0, 3):
        def rim_columns(fs, x=x):
            acc = [partial[x, c, fs, :] for c in range(4)]
            acc = columns_part(point, tab_out, rows_of[x], (0, 3), fs, acc)
            for c in range(4):
                if x in (1, 2):
                    at = c * 256 + (x - 1) * 128
                    xt[fs, at:at + 128] = normal(acc[c], fs)
                else:
                    partial[x, c, fs, :] = acc[c]

        chunks(rim_columns, 32)

    for c in weights:
        c.wait()
    network(xt, wi_out, wh_out, wo_out, bh_out, bo_out, cnt_out, tend, (1, 2), ((0, 1), (2, 3)))
    for g, x in enumerate((1, 2)):
        def store(n, fs, v, g=g):
            inner_out[g, n, fs, :] = v

        back_loop(a_out, tab_out, tend, g, x, 4, store)

    for c in jac_strip:
        c.wait_recv()
    masses_mid((0, 12))
    masses_rim((0, 12))
    for c in y_diag:
        c.wait_recv()
    sort_rows(1)
    sort_rows(2)
    halos((0, 12))
    for c in edge_copies:
        c.wait_recv()

    def assemble_outer(fs):
        h = halo[fs, :]
        for g, (level, i) in enumerate(((0, 0), (12, 3))):
            made = assemble_mid(level, fs) | assemble_rim(level, fs, h)
            acc = [partial[3 * g, c, fs, :] for c in range(4)]
            acc = columns_part(lambda p, fs: made[p], tab_out, [(i, level)], range(4), fs, acc)
            for c in range(4):
                at = c * 256 + g * 128
                xt_out[fs, at:at + 128] = normal(acc[c], fs)

    chunks(assemble_outer, 64)
    for c in copies:
        c.wait_send()


def physics_kernel(a, wi, wh, wo, bh, bo, tab, cnt, xt, inner, out, tend, obuf, out_sem):
    copies = []

    def send(src, n, x):
        c = pltpu.make_async_copy(src, out.at[:, n, x, :], out_sem.at[len(copies)])
        c.start(priority=1)
        copies.append(c)

    for g, x in enumerate((1, 2)):
        for n in range(16):
            send(inner.at[g, n], n, x)
    def row_copy(g, n):
        return pltpu.make_async_copy(obuf.at[g, n], out.at[:, n, 3 * g, :], out_sem.at[32 + g * 16 + n])

    def rest(parts):
        network(xt, wi, wh, wo, bh, bo, cnt, tend, (0, 3), parts)
        cells = sum(parts, ())
        for g in range(2):
            def back(n, carry):
                for h in range(2):
                    fs = pl.ds(h * 64, 64)
                    v = a[g * 36 + n, fs, :]
                    for c in cells:
                        v = v + tab[1, pl.ds(c * 16 + n, 1)] * tend[g, c, fs, :]
                    obuf[g, n, fs, :] = v
                row_copy(g, n).start()
                return carry

            lax.fori_loop(0, 16, back, 0)

    many = jnp.max(cnt[...]) > F32(1024.0)

    @pl.when(many)
    def _():
        rest(((0, 1), (2, 3)))

    @pl.when(jnp.logical_not(many))
    def _():
        rest(((0,), (1,)))

    copies.extend(row_copy(g, n) for g in range(2) for n in range(16))
    for c in copies:
        c.wait()


def body(
    state, wind_x, wind_y, jacobian, to_physics, to_dynamics, feature_mean, feature_scale,
    w_in, w_hidden, w_out, bias_hidden, bias_out, live_counts,
):
    n_strip, n_band = lax.axis_size("strip"), lax.axis_size("band")
    hbm = pl.BlockSpec(memory_space=pltpu.HBM)
    vmem = pl.BlockSpec(memory_space=pltpu.VMEM)
    args = (
        state.reshape(128, 16, 4, 128), wind_x.reshape(64, 128), wind_y.reshape(64, 128),
        jacobian.reshape(4, 16, 128), to_physics, to_dynamics.T, feature_mean, feature_scale,
        w_in, w_hidden, w_out, bias_hidden, bias_out.reshape(1, 128), live_counts.T,
    )
    args = [pltpu.with_memory_space_constraint(v, pltpu.HBM) for v in args]
    dma = pltpu.SemaphoreType.DMA
    made = pl.pallas_call(
        lambda *refs: exchange_kernel(n_strip, n_band, *refs),
        out_shape=[
            pltpu.VMEM((52, 128, 128), F32),
            pltpu.VMEM((128, 512), BF16),
            pltpu.VMEM((4, 512, 512), BF16),
            pltpu.VMEM((512, 128), BF16),
            pltpu.VMEM((5, 512), F32),
            pltpu.VMEM((1, 128), F32),
            pltpu.VMEM((2, 64, 128), F32),
            pltpu.VMEM((8, 128), F32),
            pltpu.VMEM((128, 1024), BF16),
            pltpu.VMEM((2, 16, 128, 128), F32),
        ],
        in_specs=[hbm] * len(args),
        out_specs=[vmem] * 10,
        scratch_shapes=[
            pltpu.VMEM((64, 128, 128), F32),
            pltpu.VMEM((64, 128), F32),
            pltpu.VMEM((64, 128), F32),
            pltpu.VMEM((4, 16, 128), F32),
            pltpu.VMEM((3, 64, 128), F32),
            pltpu.VMEM((64, 128, 128), F32),
            pltpu.VMEM((2, 4, 128, 128), BF16),
            pltpu.VMEM((2, 4, 128, 128), BF16),
            pltpu.VMEM((128, 2048), F32),
            pltpu.VMEM((32, 2048), BF16),
            pltpu.VMEM((32, 128), BF16),
            pltpu.VMEM((6, 32, 128), BF16),
            pltpu.VMEM((2, 16, 128), F32),
            pltpu.VMEM((2, 4, 8, 128), F32),
            pltpu.VMEM((4, 8, 128), F32),
            pltpu.VMEM((96, 128), F32),
            pltpu.VMEM((128, 128), F32),
            pltpu.VMEM((52, 128), F32),
            pltpu.VMEM((2, 128, 128), F32),
            pltpu.VMEM((4, 4, 128, 128), F32),
            pltpu.VMEM((128, 1024), BF16),
            pltpu.VMEM((2, 4, 128, 128), F32),
            pltpu.SMEM((4, 16), F32),
            pltpu.SMEM((4, 16), F32),
            pltpu.SMEM((n_band, n_strip), jnp.int32),
            pltpu.VMEM((2, 128), F32),
            dma((64,)),
            dma((10,)),
            dma((3,)),
            dma((16,)),
            dma((16,)),
        ],
        name="exchange",
        compiler_params=pltpu.CompilerParams(
            collective_id=0, has_side_effects=True, vmem_limit_bytes=32 << 20
        ),
    )(*args)
    out = pl.pallas_call(
        physics_kernel,
        out_shape=jax.ShapeDtypeStruct((128, 16, 4, 128), F32),
        in_specs=[vmem] * 10,
        out_specs=hbm,
        scratch_shapes=[
            pltpu.VMEM((2, 4, 128, 128), F32),
            pltpu.VMEM((2, 16, 128, 128), F32),
            dma((64,)),
        ],
        name="physics",
        compiler_params=pltpu.CompilerParams(vmem_limit_bytes=28 << 20),
    )(*made)
    return out.reshape(state.shape)


def solution(mesh):
    placed = (
        P(None, None, None, "strip", "band"),
        P(None, None, "strip", "band"),
        P(None, None, "strip", "band"),
        P(None, None, "strip", "band"),
        P(), P(), P(), P(), P(), P(), P(), P(), P(), P(),
    )
    return jax.shard_map(
        body,
        mesh=mesh,
        in_specs=placed,
        out_specs=P(None, None, None, "strip", "band"),
        check_vma=False,
    )
```

```python
import jax
import jax.numpy as jnp
import numpy as np
from jax import lax
from jax.experimental import pallas as pl
from jax.experimental.pallas import tpu as pltpu
from jax.sharding import PartitionSpec as P

MESH = pl.DeviceIdType.MESH
step_size = 0.1
slope = 0.15
F32 = jnp.float32
BF16 = jnp.bfloat16


def gll_tables():
    nodes = np.array([-1.0, -1.0 / np.sqrt(5.0), 1.0 / np.sqrt(5.0), 1.0])
    weights = np.array([1.0 / 6.0, 5.0 / 6.0, 5.0 / 6.0, 1.0 / 6.0])
    derivative = np.zeros((4, 4))
    for first in range(4):
        for second in range(4):
            if first != second:
                top = np.prod([nodes[first] - nodes[other] for other in range(4) if other != first])
                bottom = np.prod(
                    [nodes[second] - nodes[other] for other in range(4) if other != second]
                )
                derivative[first, second] = top / (bottom * (nodes[first] - nodes[second]))
            else:
                derivative[first, first] = np.sum(
                    [1.0 / (nodes[first] - nodes[other]) for other in range(4) if other != first]
                )
    return (weights, derivative)


WEIGHTS, DERIV = gll_tables()
QUAD = np.outer(WEIGHTS, WEIGHTS)
EVEN = [(DERIV[r, 0] + DERIV[r, 3]) / 2 for r in (0, 1)]
ODD0 = [(DERIV[r, 0] - DERIV[r, 3]) / 2 for r in (0, 1)]
ODD1 = [(DERIV[r, 1] - DERIV[r, 2]) / 2 for r in (0, 1)]
LEAD = [ODD0[0], ODD1[1], ODD1[1], ODD0[0]]


def mirrored(s0, s1, s2, s3):
    even = (s0 + s3) - (s1 + s2)
    far, near = s0 - s3, s1 - s2
    outer = far + F32(ODD1[0] / ODD0[0]) * near
    inner = near + F32(ODD0[1] / ODD1[1]) * far
    outer_e = F32(EVEN[0] / ODD0[0]) * even
    inner_e = F32(EVEN[1] / ODD1[1]) * even
    return outer + outer_e, inner + inner_e, inner - inner_e, outer - outer_e


def lanes(rows):
    return lax.broadcasted_iota(jnp.int32, (rows, 128), 1)


def columns_part(a_of, tab, levels, nodes, fs, acc):
    for i, level in levels:
        for j in nodes:
            v = a_of(level * 4 + j, fs)
            for c in range(4):
                r = c * 16 + i * 4 + j
                term = tab[0, r:r + 1] * v
                acc[c] = term if acc[c] is None else acc[c] + term
    return acc


def network(xt, wi, wh, wo, bh, bo, cnt, tend, xs, parts):
    lane = lanes(1).astype(F32)

    def act(acc, bias):
        v = acc + bias
        return jnp.maximum(v, F32(slope) * v).astype(BF16)

    def dot(p, q):
        return jnp.dot(p, q, preferred_element_type=F32)

    hs = [act(dot(xt[:, p[0] * 256:(p[-1] + 1) * 256].T, wi[...]), bh[0:1]) for p in parts]
    for layer in range(4):
        hs = [act(dot(h, wh[layer]), bh[layer + 1:layer + 2]) for h in hs]
    for p, h in zip(parts, hs):
        raw = (dot(h, wo[...]) + bo[...]).astype(BF16).T
        for c in p:
            for g in range(2):
                live = lane + F32(c * 512 + xs[g] * 128) < cnt[0:1]
                at = ((c - p[0]) * 2 + g) * 128
                tend[g, c] = jnp.where(live, raw[:, at:at + 128].astype(F32), F32(0.0))


def back_loop(a, tab, tend, g, x, cells, store):
    def back(k, carry):
        fs = pl.ds(pl.multiple_of(k * 64, 64), 64)
        t = [tend[g, c, fs, :] for c in range(cells)]
        for n in range(16):
            v = a[(3 * x + n // 4) * 4 + n % 4, fs, :]
            for c in range(cells):
                v = v + tab[1, c * 16 + n:c * 16 + n + 1] * t[c]
            store(n, fs, v)
        return carry

    lax.fori_loop(0, 2, back, 0)


def exchange_kernel(
    n_strip, n_band,
    state, wind_x, wind_y, jac, to_phys, to_dyn, mean, scale, w_in, w_hidden, w_out, bias_h, bias_o, counts,
    a_out, wi_out, wh_out, wo_out, bh_out, bo_out, tab_out, cnt_out, xt_out, inner_out,
    sbuf, wxv, wyv, jacv, coef, qbuf, edge_send, edge_recv, pack, pick, ysend, yrecv,
    jstrip, jband, jdiag, gather, halo, rmass, norm, partial, xt, tend, tp_s, td_s, cnt_s, rowv,
    in_sem, small_sem, w_sem, send_sem, recv_sem,
):
    s = lax.axis_index("strip")
    b = lax.axis_index("band")
    sp, sm = lax.rem(s + 1, n_strip), lax.rem(s + n_strip - 1, n_strip)
    bp, bm = lax.rem(b + 1, n_band), lax.rem(b + n_band - 1, n_band)

    def state_copy(n, x):
        return pltpu.make_async_copy(state.at[:, n, x, :], sbuf.at[n * 4 + x], in_sem.at[n * 4 + x])

    def local(src, dst, sem, priority=0):
        c = pltpu.make_async_copy(src, dst, sem)
        c.start(priority=priority)
        return c

    small = [
        local(jac, jacv, small_sem.at[0]),
        local(wind_x, wxv, small_sem.at[1]),
        local(wind_y, wyv, small_sem.at[2]),
    ]
    for n in range(16):
        state_copy(n, 0).start()
    barrier = pltpu.get_barrier_semaphore()
    for dev in ((sp, b), (sm, b), (s, bp), (s, bm), (sp, bp), (sp, bm), (sm, bp), (sm, bm)):
        pl.semaphore_signal(barrier, inc=1, device_id=dev, device_id_type=MESH)
    for x in range(1, 4):
        for n in range(16):
            state_copy(n, x).start(priority=1)

    copies = []

    def remote(src, dst, dev):
        n = len(copies)
        c = pltpu.make_async_remote_copy(
            src_ref=src, dst_ref=dst, send_sem=send_sem.at[n], recv_sem=recv_sem.at[n],
            device_id=dev, device_id_type=MESH,
        )
        copies.append(c)
        return c

    top, low = pl.ds(8, 8), pl.ds(0, 8)
    jac_band = [
        remote(jacv.at[:, top], jband.at[0], (s, bp)),
        remote(jacv.at[:, low], jband.at[1], (s, bm)),
    ]
    jac_strip = [
        remote(jacv.at[3], jstrip.at[0], (sp, b)),
        remote(jacv.at[0], jstrip.at[1], (sm, b)),
        remote(jacv.at[3, top], jdiag.at[0], (sp, bp)),
        remote(jacv.at[3, low], jdiag.at[1], (sp, bm)),
        remote(jacv.at[0, top], jdiag.at[2], (sm, bp)),
        remote(jacv.at[0, low], jdiag.at[3], (sm, bm)),
    ]
    halves = [pl.ds(0, 64), pl.ds(64, 64)]
    edge_copies = [
        [
            remote(edge_send.at[0, :, h], edge_recv.at[0, :, h], (sp, b)),
            remote(edge_send.at[1, :, h], edge_recv.at[1, :, h], (sm, b)),
        ]
        for h in halves
    ]
    y_band = [
        remote(ysend, yrecv.at[0], (s, bp)),
        remote(ysend, yrecv.at[1], (s, bm)),
    ]
    y_diag = [
        remote(ysend, yrecv.at[2], (sp, bp)),
        remote(ysend, yrecv.at[3], (sp, bm)),
        remote(ysend, yrecv.at[4], (sm, bp)),
        remote(ysend, yrecv.at[5], (sm, bm)),
    ]

    wide = (32, 2048)
    row, col = (lax.broadcasted_iota(jnp.int32, wide, d) for d in (0, 1))
    at = (row // 2) * 128 + jnp.where(lax.rem(row, 2) == 0, 127, 0)
    pick[...] = jnp.where(col == at, F32(1.0), F32(0.0)).astype(BF16)

    for c in small:
        c.wait()
    for i in range(4):
        for jp in range(2):
            at = slice(i * 16 + jp * 8, i * 16 + jp * 8 + 8)
            first = lax.broadcasted_iota(jnp.int32, (8, 128), 0) < 4
            j0, j1 = 2 * jp, 2 * jp + 1
            m = jacv[i, jp * 8:jp * 8 + 8] * jnp.where(first, F32(QUAD[i, j0]), F32(QUAD[i, j1]))
            coef[0, at] = m
            coef[1, at] = m * wxv[at] * F32(-step_size * LEAD[i])
            lead = jnp.where(first, F32(-step_size * LEAD[j0]), F32(-step_size * LEAD[j1]))
            coef[2, at] = m * wyv[at] * lead

    lane = lanes(16)

    def advect_column(x):
        for n in range(16):
            state_copy(n, x).wait()

        def advect(k, carry):
            fs = pl.ds(pl.multiple_of(k * 16, 16), 16)
            v = [[sbuf[i * 16 + j * 4 + x, fs, :] for j in range(4)] for i in range(4)]
            q = [[None] * 4 for _ in range(4)]
            for j in range(4):
                d = mirrored(*[v[i][j] for i in range(4)])
                for i in range(4):
                    r = i * 16 + j * 4 + x
                    q[i][j] = coef[0, r:r + 1] * v[i][j] + coef[1, r:r + 1] * d[i]
            for i in range(4):
                d = mirrored(*v[i])
                for j in range(4):
                    r = i * 16 + j * 4 + x
                    q[i][j] = q[i][j] + coef[2, r:r + 1] * d[j]
                    qbuf[r, fs, :] = q[i][j]
                n = i * 4 + x
                pack[fs, n * 128:n * 128 + 128] = jnp.where(lane == 127, q[i][3], q[i][0])
            return carry

        lax.fori_loop(0, 8, advect, 0)

    advect_column(0)
    for j in range(4):
        edge_send[1, j] = qbuf[j * 4].astype(BF16)
    advect_column(1)
    later = [
        local(to_phys, tp_s, small_sem.at[3]),
        local(to_dyn, td_s, small_sem.at[4]),
        local(counts, cnt_s, small_sem.at[5]),
        local(mean, rowv.at[0], small_sem.at[6]),
        local(scale, rowv.at[1], small_sem.at[7]),
        local(bias_h, bh_out, small_sem.at[8]),
        local(bias_o, bo_out, small_sem.at[9]),
    ]
    weights = [
        local(w_in, wi_out, w_sem.at[0], 1),
        local(w_hidden, wh_out, w_sem.at[1], 1),
        local(w_out, wo_out, w_sem.at[2], 1),
    ]
    advect_column(2)
    advect_column(3)
    for j in range(4):
        edge_send[0, j] = qbuf[48 + j * 4 + 3].astype(BF16)
    ysend[...] = lax.dot_general(
        pick[...], pack[...].astype(BF16), (((1,), (1,)), ((), ())), preferred_element_type=F32
    ).astype(BF16)
    pl.semaphore_wait(barrier, 8)
    for c in y_band + jac_band + y_diag + jac_strip + edge_copies[0] + edge_copies[1]:
        c.start()

    for c in later:
        c.wait()
    for c in range(4):
        for n in range(16):
            tab_out[0, pl.ds(c * 16 + n, 1)] = jnp.full((1, 128), tp_s[c, n], F32)
            tab_out[1, pl.ds(c * 16 + n, 1)] = jnp.full((1, 128), td_s[c, n], F32)
    norm[0] = jnp.broadcast_to(rowv[0:1], (128, 128)).T
    norm[1] = jnp.broadcast_to(rowv[1:2], (128, 128)).T
    cnt_out[...] = jnp.full((8, 128), cnt_s[b, s].astype(F32), F32)

    lane1 = lanes(1)

    def element(side, i, j, x):
        w = F32(QUAD[i, j])
        r = j * 4 + x
        if side is None:
            return coef[0, i * 16 + r:i * 16 + r + 1]
        r = r - 8 if side == 0 else r
        return w * jband[side, i, r:r + 1]

    def outer(strip_side, band_side, j):
        i, x = (3, 3) if strip_side == 0 else (0, 0)
        w = F32(QUAD[i, j])
        r = j * 4 + x
        if band_side is None:
            return w * jstrip[strip_side, r:r + 1]
        r = r - 8 if band_side == 0 else r
        return w * jdiag[strip_side * 2 + band_side, r:r + 1]

    def level_mass(level, side, j):
        if level == 0:
            return element(side, 0, j, 0) + outer(0, side, j)
        if level == 12:
            return element(side, 3, j, 3) + outer(1, side, j)
        x, i = divmod(level, 3)
        if i == 0:
            return element(side, 0, j, x) + element(side, 3, j, x - 1)
        return element(side, i, j, x)

    def masses_mid(levels):
        for level in levels:
            for j in (1, 2):
                rmass[pl.ds(level * 4 + j, 1)] = 1.0 / level_mass(level, None, j)

    def masses_rim(levels):
        for level in levels:
            m = {j: level_mass(level, None, j) for j in (0, 3)}
            before = jnp.where(lane1 == 127, level_mass(level, 0, 3), m[3])
            after = jnp.where(lane1 == 0, level_mass(level, 1, 0), m[0])
            rmass[pl.ds(level * 4, 1)] = 1.0 / (m[0] + pltpu.roll(before, 1, 1))
            rmass[pl.ds(level * 4 + 3, 1)] = 1.0 / (m[3] + pltpu.roll(after, 127, 1))

    odd = lax.rem(lax.broadcasted_iota(jnp.int32, (32, 128), 0), 2) == 1

    def sort_rows(t):
        from_left = pltpu.roll(yrecv[2 * t].astype(F32), 1, 0)
        from_right = pltpu.roll(yrecv[2 * t + 1].astype(F32), 31, 0)
        gather[t * 32:(t + 1) * 32] = jnp.where(odd, from_left, from_right)

    def pair(t, i, x):
        r = t * 32 + 2 * (i * 4 + x)
        return gather[r:r + 2]

    def level_rows(level):
        x, i = divmod(level, 3)
        if level == 0:
            return pair(0, 0, 0) + pair(1, 3, 3)
        if level == 12:
            return pair(0, 3, 3) + pair(2, 0, 0)
        if i == 0:
            return pair(0, 0, x) + pair(0, 3, x - 1)
        return pair(0, i, x)

    def halos(levels):
        halo[...] = jnp.zeros((128, 128), F32)
        for level in levels:
            halo[2 * level:2 * level + 2] = level_rows(level)
        halo[...] = halo[...].T

    def strip_sum(level, j, fs):
        x, i = divmod(level, 3)
        if level == 12:
            return qbuf[48 + j * 4 + 3, fs, :] + edge_recv[1, j, fs, :].astype(F32)
        u = qbuf[i * 16 + j * 4 + x, fs, :]
        if level == 0:
            return u + edge_recv[0, j, fs, :].astype(F32)
        return u + qbuf[48 + j * 4 + x - 1, fs, :] if i == 0 else u

    def assemble_mid(level, fs):
        made = {}
        for j in (1, 2):
            p = level * 4 + j
            made[p] = strip_sum(level, j, fs) * rmass[p:p + 1]
            a_out[p, fs, :] = made[p]
        return made

    def assemble_rim(level, fs, h):
        low, high = strip_sum(level, 0, fs), strip_sum(level, 3, fs)
        lane = lanes(low.shape[0])
        hr = pltpu.roll(h, 128 - (2 * level + 1), 1)
        first = low + jnp.where(lane == 0, hr, pltpu.roll(high, 1, 1))
        last = high + jnp.where(lane == 127, hr, pltpu.roll(low, 127, 1))
        p = level * 4
        made = {p: first * rmass[p:p + 1], p + 3: last * rmass[p + 3:p + 4]}
        a_out[p, fs, :] = made[p]
        a_out[p + 3, fs, :] = made[p + 3]
        return made

    def chunks(step, size):
        def run(k, carry):
            step(pl.ds(pl.multiple_of(k * size, size), size))
            return carry

        lax.fori_loop(0, 128 // size, run, 0)

    def point(p, fs):
        return a_out[p, fs, :]

    def normal(v, fs):
        return ((v - norm[0, fs, :]) * norm[1, fs, :]).astype(BF16)

    inner = range(1, 12)
    rows_of = {x: [(i, 3 * x + i) for i in range(4) if 3 * x + i in inner] for x in range(4)}

    masses_mid(inner)

    def mid(fs):
        for level in inner:
            assemble_mid(level, fs)

    chunks(mid, 64)
    for x in range(4):
        def mid_columns(fs, x=x):
            acc = columns_part(point, tab_out, rows_of[x], (1, 2), fs, [None] * 4)
            for c in range(4):
                partial[x, c, fs, :] = acc[c]

        chunks(mid_columns, 32)

    for c in jac_band:
        c.wait_recv()
    masses_rim(inner)
    for c in y_band:
        c.wait_recv()
    sort_rows(0)
    halos(inner)

    def rim(fs):
        h = halo[fs, :]
        for level in inner:
            assemble_rim(level, fs, h)

    chunks(rim, 64)
    for x in (1, 2, 0, 3):
        def rim_columns(fs, x=x):
            acc = [partial[x, c, fs, :] for c in range(4)]
            acc = columns_part(point, tab_out, rows_of[x], (0, 3), fs, acc)
            for c in range(4):
                if x in (1, 2):
                    at = c * 256 + (x - 1) * 128
                    xt[fs, at:at + 128] = normal(acc[c], fs)
                else:
                    partial[x, c, fs, :] = acc[c]

        chunks(rim_columns, 32)

    for c in weights:
        c.wait()
    network(xt, wi_out, wh_out, wo_out, bh_out, bo_out, cnt_out, tend, (1, 2), ((0, 1), (2, 3)))
    for g, x in enumerate((1, 2)):
        def store(n, fs, v, g=g):
            inner_out[g, n, fs, :] = v

        back_loop(a_out, tab_out, tend, g, x, 4, store)

    for c in jac_strip:
        c.wait_recv()
    masses_mid((0, 12))
    masses_rim((0, 12))
    for c in y_diag:
        c.wait_recv()
    sort_rows(1)
    sort_rows(2)
    halos((0, 12))

    def assemble_outer(fs):
        h = halo[fs, :]
        for g, (level, i) in enumerate(((0, 0), (12, 3))):
            made = assemble_mid(level, fs) | assemble_rim(level, fs, h)
            acc = [partial[3 * g, c, fs, :] for c in range(4)]
            acc = columns_part(lambda p, fs: made[p], tab_out, [(i, level)], range(4), fs, acc)
            for c in range(4):
                at = c * 256 + g * 128
                xt_out[fs, at:at + 128] = normal(acc[c], fs)

    for half, pair_of in zip(halves, edge_copies):
        for c in pair_of:
            c.wait_recv()
        assemble_outer(half)
    for c in copies:
        c.wait_send()


def physics_kernel(a, wi, wh, wo, bh, bo, tab, cnt, xt, inner, out, tend, obuf, out_sem):
    copies = []

    def send(src, n, x):
        c = pltpu.make_async_copy(src, out.at[:, n, x, :], out_sem.at[len(copies)])
        c.start(priority=1)
        copies.append(c)

    for g, x in enumerate((1, 2)):
        for n in range(16):
            send(inner.at[g, n], n, x)
    def row_copy(g, n):
        return pltpu.make_async_copy(obuf.at[g, n], out.at[:, n, 3 * g, :], out_sem.at[32 + g * 16 + n])

    def rest(parts):
        network(xt, wi, wh, wo, bh, bo, cnt, tend, (0, 3), parts)
        cells = sum(parts, ())
        for g in range(2):
            def back(n, carry):
                for h in range(2):
                    fs = pl.ds(h * 64, 64)
                    v = a[g * 36 + n, fs, :]
                    for c in cells:
                        v = v + tab[1, pl.ds(c * 16 + n, 1)] * tend[g, c, fs, :]
                    obuf[g, n, fs, :] = v
                row_copy(g, n).start()
                return carry

            lax.fori_loop(0, 16, back, 0)

    count = jnp.max(cnt[...])
    many, few = count > F32(1024.0), count <= F32(512.0)

    @pl.when(many)
    def _():
        rest(((0, 1), (2, 3)))

    @pl.when(few)
    def _():
        rest(((0,),))

    @pl.when(jnp.logical_not(jnp.logical_or(many, few)))
    def _():
        rest(((0,), (1,)))

    copies.extend(row_copy(g, n) for g in range(2) for n in range(16))
    for c in copies:
        c.wait()


def body(
    state, wind_x, wind_y, jacobian, to_physics, to_dynamics, feature_mean, feature_scale,
    w_in, w_hidden, w_out, bias_hidden, bias_out, live_counts,
):
    n_strip, n_band = lax.axis_size("strip"), lax.axis_size("band")
    hbm = pl.BlockSpec(memory_space=pltpu.HBM)
    vmem = pl.BlockSpec(memory_space=pltpu.VMEM)
    args = (
        state.reshape(128, 16, 4, 128), wind_x.reshape(64, 128), wind_y.reshape(64, 128),
        jacobian.reshape(4, 16, 128), to_physics, to_dynamics.T, feature_mean, feature_scale,
        w_in, w_hidden, w_out, bias_hidden, bias_out.reshape(1, 128), live_counts.T,
    )
    args = [pltpu.with_memory_space_constraint(v, pltpu.HBM) for v in args]
    dma = pltpu.SemaphoreType.DMA
    made = pl.pallas_call(
        lambda *refs: exchange_kernel(n_strip, n_band, *refs),
        out_shape=[
            pltpu.VMEM((52, 128, 128), F32),
            pltpu.VMEM((128, 512), BF16),
            pltpu.VMEM((4, 512, 512), BF16),
            pltpu.VMEM((512, 128), BF16),
            pltpu.VMEM((5, 512), F32),
            pltpu.VMEM((1, 128), F32),
            pltpu.VMEM((2, 64, 128), F32),
            pltpu.VMEM((8, 128), F32),
            pltpu.VMEM((128, 1024), BF16),
            pltpu.VMEM((2, 16, 128, 128), F32),
        ],
        in_specs=[hbm] * len(args),
        out_specs=[vmem] * 10,
        scratch_shapes=[
            pltpu.VMEM((64, 128, 128), F32),
            pltpu.VMEM((64, 128), F32),
            pltpu.VMEM((64, 128), F32),
            pltpu.VMEM((4, 16, 128), F32),
            pltpu.VMEM((3, 64, 128), F32),
            pltpu.VMEM((64, 128, 128), F32),
            pltpu.VMEM((2, 4, 128, 128), BF16),
            pltpu.VMEM((2, 4, 128, 128), BF16),
            pltpu.VMEM((128, 2048), F32),
            pltpu.VMEM((32, 2048), BF16),
            pltpu.VMEM((32, 128), BF16),
            pltpu.VMEM((6, 32, 128), BF16),
            pltpu.VMEM((2, 16, 128), F32),
            pltpu.VMEM((2, 4, 8, 128), F32),
            pltpu.VMEM((4, 8, 128), F32),
            pltpu.VMEM((96, 128), F32),
            pltpu.VMEM((128, 128), F32),
            pltpu.VMEM((52, 128), F32),
            pltpu.VMEM((2, 128, 128), F32),
            pltpu.VMEM((4, 4, 128, 128), F32),
            pltpu.VMEM((128, 1024), BF16),
            pltpu.VMEM((2, 4, 128, 128), F32),
            pltpu.SMEM((4, 16), F32),
            pltpu.SMEM((4, 16), F32),
            pltpu.SMEM((n_band, n_strip), jnp.int32),
            pltpu.VMEM((2, 128), F32),
            dma((64,)),
            dma((10,)),
            dma((3,)),
            dma((18,)),
            dma((18,)),
        ],
        name="exchange",
        compiler_params=pltpu.CompilerParams(
            collective_id=0, has_side_effects=True, vmem_limit_bytes=32 << 20
        ),
    )(*args)
    out = pl.pallas_call(
        physics_kernel,
        out_shape=jax.ShapeDtypeStruct((128, 16, 4, 128), F32),
        in_specs=[vmem] * 10,
        out_specs=hbm,
        scratch_shapes=[
            pltpu.VMEM((2, 4, 128, 128), F32),
            pltpu.VMEM((2, 16, 128, 128), F32),
            dma((64,)),
        ],
        name="physics",
        compiler_params=pltpu.CompilerParams(vmem_limit_bytes=28 << 20),
    )(*made)
    return out.reshape(state.shape)


def solution(mesh):
    placed = (
        P(None, None, None, "strip", "band"),
        P(None, None, "strip", "band"),
        P(None, None, "strip", "band"),
        P(None, None, "strip", "band"),
        P(), P(), P(), P(), P(), P(), P(), P(), P(), P(),
    )
    return jax.shard_map(
        body,
        mesh=mesh,
        in_specs=placed,
        out_specs=P(None, None, None, "strip", "band"),
        check_vma=False,
    )
```
